32 devices in a mesh: seq: 8 (over z, y), mlp: 4 (over x, core).
Axes of the slice: x: 2, y: 2, z: 4, core: 2. Of those that a mesh axis runs over, the one named last changes fastest.
Arguments:
- tokens: bfloat16 [4096, 768], P('seq'), may hold values from -6 to 6
- cotangent: bfloat16 [4096, 768], P('seq'), may hold values from -6 to 6
- picks: int32 [16, 128], P('seq'), may hold values from 0 to 255, as said below
- eighths: int32 [16], replicated, may hold values from 1 to 4, as said below
- w_router: bfloat16 [768], replicated, may hold values from -0.21875 to 0.21875
- gain_attn: bfloat16 [768], replicated, may hold values from 0.25 to 1.75
- gain_mlp: bfloat16 [768], replicated, may hold values from 0.25 to 1.75
- w_query: bfloat16 [768, 768], replicated, may hold values from -0.21875 to 0.21875
- w_key: bfloat16 [768, 768], replicated, may hold values from -0.21875 to 0.21875
- w_value: bfloat16 [768, 768], replicated, may hold values from -0.21875 to 0.21875
- w_out: bfloat16 [768, 768], replicated, may hold values from -0.875 to 0.875
- w_up: bfloat16 [768, 3072], P(None, 'mlp'), may hold values from -0.21875 to 0.21875
- w_down: bfloat16 [3072, 768], P('mlp'), may hold values from -0.109375 to 0.109375
Outputs:
- mixed: bfloat16 [4096, 768], P('seq')
- grad_tokens: bfloat16 [4096, 768], P('seq')
- grad_router: float32 [768], replicated
- grad_gain_attn: float32 [768], replicated
- grad_gain_mlp: float32 [768], replicated
- grad_query: float32 [768, 768], replicated
- grad_key: float32 [768, 768], replicated
- grad_value: float32 [768, 768], replicated
- grad_out: float32 [768, 768], replicated
- grad_up: float32 [768, 3072], P(None, 'mlp')
- grad_down: float32 [3072, 768], P('mlp')
The draws below stay inside these ranges and needn't reach their ends.
Inputs may be any that keep to these rules, and one draw needn't show every extreme that they name: `eighths`: each is 1, 2 or 4. In each aligned group of 8 sequences (sequences 8 g to 8 g + 7) the values are 4, 4, 2, 2, 1, 1, 1, 1 in some order. `picks`: row s lists in increasing order the eighths[s] * 32 distinct positions of the selected tokens of sequence s, followed by zeros.
All inputs are finite; a program needn't handle non-finite values.
Results may differ from the reference program's by a relative error of at most 0.012.
Values may be sent and summed in bfloat16 or wider, within the bound.
No kernel may reach another device: no remote copies, remote signals or barrier semaphores. Data moves between devices by JAX's collectives and lax.ppermute only.
A program may use at most 128 MiB of HBM per device.

```python
import jax
import jax.numpy as jnp
from jax import lax

D = 768
HEADS = 12
HEAD = 64
FF = 3072
LEN = 256
SEQS = 16
TOKENS = 4096
CAP = 128


def share_table(key):
    share_pattern = jnp.array([4, 4, 2, 2, 1, 1, 1, 1], jnp.int32)
    group_keys = jax.random.split(jax.random.fold_in(key, 101), SEQS // 8)

    def shuffle_one(group_key):
        return jax.random.permutation(group_key, share_pattern)
    return jax.vmap(shuffle_one)(group_keys).reshape(SEQS).astype(jnp.int32)


def draw_eighths(key, part):
    return share_table(key)


def draw_picks(key, part):
    needed_rows = share_table(key) * (LEN // 8)
    row_keys = jax.random.split(jax.random.fold_in(key, 202), SEQS)

    def one_row(row_key, needed):
        shuffled = jax.random.permutation(row_key, LEN).astype(jnp.int32)
        rank_of = jnp.argsort(shuffled).astype(jnp.int32)
        chosen = rank_of < needed
        listing = jnp.argsort(jnp.where(chosen, 0, 1).astype(jnp.int32), stable=True).astype(jnp.int32)[:LEN // 2]
        return jnp.where(jnp.arange(LEN // 2, dtype=jnp.int32) < needed, listing, 0)
    return jax.vmap(one_row)(row_keys, needed_rows).astype(jnp.int32)


def block_scale(stream_key, dims, shards, smallest, largest):
    level, own = 1.0, jax.random.fold_in(stream_key, 6)
    for axis_at, parts in shards:
        draws = jnp.exp(jax.random.uniform(jax.random.fold_in(own, axis_at), (parts,), jnp.float32, smallest / len(shards), largest / len(shards)))
        level = level * jnp.repeat(draws, dims[axis_at] // parts).reshape([-1 if axis == axis_at else 1 for axis in range(len(dims))])
    return level


def normal_values(own_key, dims, width, reach, shards=(), kind=jnp.bfloat16):
    loudness = block_scale(own_key, dims, shards, -0.22, 0.18) if shards else 1.0
    result = jax.random.normal(own_key, dims, jnp.float32) * width * loudness
    return jnp.minimum(jnp.maximum(result, -reach), reach).astype(kind)


def setup_inputs(seed: int = 0) -> dict:
    seeds = jax.random.split(jax.random.key(seed), 14)
    tokens = normal_values(seeds[0], (TOKENS, D), 1.0, 6.0, ((0, 8),))
    cotangent = normal_values(seeds[1], (TOKENS, D), 1.0, 6.0, ((0, 8),))
    picks = draw_picks(jax.random.fold_in(seeds[13], 71), 0)
    eighths = draw_eighths(jax.random.fold_in(seeds[13], 71), 0)
    w_router = normal_values(seeds[4], (D,), D ** -0.5, 0.21875)
    gain_attn = jnp.clip(1.0 + 0.15 * jax.random.normal(seeds[5], (D,), jnp.float32), 0.25, 1.75).astype(jnp.bfloat16)
    gain_mlp = jnp.clip(1.0 + 0.15 * jax.random.normal(seeds[6], (D,), jnp.float32), 0.25, 1.75).astype(jnp.bfloat16)
    w_query = normal_values(seeds[7], (D, D), D ** -0.5, 0.21875)
    w_key = normal_values(seeds[8], (D, D), D ** -0.5, 0.21875)
    w_value = normal_values(seeds[9], (D, D), D ** -0.5, 0.21875)
    w_out = normal_values(seeds[10], (D, D), (D // 16) ** -0.5, 0.875)
    w_up = normal_values(seeds[11], (D, FF), D ** -0.5, 0.21875, ((1, 4),))
    w_down = normal_values(seeds[12], (FF, D), FF ** -0.5, 0.109375, ((0, 4),))
    return {"tokens": tokens, "cotangent": cotangent, "picks": picks, "eighths": eighths, "w_router": w_router, "gain_attn": gain_attn, "gain_mlp": gain_mlp, "w_query": w_query, "w_key": w_key, "w_value": w_value, "w_out": w_out, "w_up": w_up, "w_down": w_down}


@jax.custom_vjp
def low(v):
    return lax.optimization_barrier(v.astype(jnp.bfloat16)).astype(jnp.float32)

@jax.custom_vjp
def low_back(v):
    return v

def low_keep(v):
    return (low(v), None)

def low_pass(kept, grad):
    return (grad,)

def back_keep(v):
    return (v, None)

def back_low(kept, grad):
    return (low(grad),)
low.defvjp(low_keep, low_pass)
low_back.defvjp(back_keep, back_low)
EPS = 1e-06
NEG = -1e+30
SCALE = 0.125

def matmul(left, right):
    return jnp.dot(left, right, preferred_element_type=jnp.float32, precision=lax.Precision.HIGHEST)

def rms_norm(values, gain):
    return values * lax.rsqrt(lax.optimization_barrier(jnp.mean(values * values, axis=-1, keepdims=True)) + EPS) * gain

def one_sequence(weights, seq_x, seq_picks, seq_rows):
    w_router, gain_attn, gain_mlp, w_query, w_key, w_value, w_out, w_up, w_down = weights
    slot_ids = jnp.arange(CAP, dtype=jnp.int32)
    in_use = slot_ids < seq_rows
    picked = jnp.where(in_use[:, None], seq_x[seq_picks], 0.0)
    gate_value = low_back(low(jnp.dot(picked, w_router, precision=lax.Precision.HIGHEST)))
    rows_in = low_back(picked)
    norm_one = low(rms_norm(rows_in, gain_attn))
    query = low(low_back(matmul(norm_one, w_query))).reshape(CAP, HEADS, HEAD)
    key_rows = low(low_back(matmul(norm_one, w_key))).reshape(CAP, HEADS, HEAD)
    value_rows = low(low_back(matmul(norm_one, w_value))).reshape(CAP, HEADS, HEAD)
    allowed = (slot_ids[None, :] <= slot_ids[:, None]) & (in_use[:, None] == in_use[None, :])
    scores = SCALE * jnp.einsum('qhd,khd->hqk', query, key_rows, precision=lax.Precision.HIGHEST, preferred_element_type=jnp.float32)
    scores = low_back(scores)
    scores = jnp.where(allowed[None], scores, NEG)
    row_peak = lax.optimization_barrier(jnp.max(scores, axis=-1, keepdims=True))
    exp_scores = jnp.exp(scores - row_peak)
    probabilities = low(exp_scores / lax.optimization_barrier(jnp.sum(exp_scores, axis=-1, keepdims=True)))
    context = jnp.einsum('hqk,khd->qhd', probabilities, value_rows, precision=lax.Precision.HIGHEST, preferred_element_type=jnp.float32)
    context = low(low_back(context.reshape(CAP, D)))
    attn_out = low_back(matmul(context, w_out))
    mid = rows_in + attn_out
    norm_two = low(rms_norm(mid, gain_mlp))
    up_pre = low_back(matmul(norm_two, w_up))
    activ = low(jax.nn.gelu(up_pre, approximate=True))
    mlp_out = low_back(matmul(activ, w_down))
    delta = low(gate_value[:, None] * (attn_out + mlp_out))
    return seq_x.at[seq_picks].add(jnp.where(in_use[:, None], delta, 0.0))

def reference(tokens, cotangent, picks, eighths, w_router, gain_attn, gain_mlp, w_query, w_key, w_value, w_out, w_up, w_down):
    weights = tuple((weight_arr.astype(jnp.float32) for weight_arr in (w_router, gain_attn, gain_mlp, w_query, w_key, w_value, w_out, w_up, w_down)))
    seq_tokens = tokens.astype(jnp.float32).reshape(SEQS, LEN, D)
    seq_rows = (eighths * (LEN // 8)).astype(jnp.int32)
    picks_int = picks.astype(jnp.int32)

    def forward(weight_set, inputs):

        def per_sequence(packed):
            return one_sequence(weight_set, packed[0], packed[1], packed[2])
        return lax.map(jax.checkpoint(per_sequence), (inputs, picks_int, seq_rows))
    outputs, pullback = jax.vjp(forward, weights, seq_tokens)
    weight_grads, input_grad = pullback(cotangent.astype(jnp.float32).reshape(SEQS, LEN, D))
    mixed = outputs.reshape(TOKENS, D).astype(jnp.bfloat16)
    grad_tokens = input_grad.reshape(TOKENS, D).astype(jnp.bfloat16)
    return (mixed, grad_tokens, weight_grads[0], weight_grads[1], weight_grads[2], weight_grads[3], weight_grads[4], weight_grads[5], weight_grads[6], weight_grads[7], weight_grads[8])
```

```python
import functools

import jax
import jax.numpy as jnp
from jax import lax
from jax.experimental import pallas as pl
from jax.experimental.pallas import tpu as pltpu
from jax.sharding import PartitionSpec as P

F32 = jnp.float32
BF = jnp.bfloat16
EPS = 1e-06
NEG = -1e30
SCALE = 0.125
D = 768
T = 128
PAIRS = 6
GROUP = 8
BLOCK = 32
MIB = 2**20


def nn(a, b):
    return lax.dot_general(a, b, (((1,), (0,)), ((), ())), preferred_element_type=F32)


def nt(a, b):
    return lax.dot_general(a, b, (((1,), (1,)), ((), ())), preferred_element_type=F32)


def tn(a, b):
    return lax.dot_general(a, b, (((0,), (0,)), ((), ())), preferred_element_type=F32)


def iota(shape, dim):
    return lax.broadcasted_iota(jnp.int32, shape, dim)


def inv_rms(v):
    return lax.rsqrt(jnp.mean(v * v, axis=-1, keepdims=True) + EPS)


def causal(span):
    rows, cols = iota((2 * T, T), 0) % T, iota((2 * T, T), 1)
    return (cols <= rows) & (rows // span == cols // span)


def two_heads(v):
    low = iota((T, T), 1) < 64
    zero = jnp.zeros((), BF)
    return jnp.concatenate([jnp.where(low, v, zero), jnp.where(low, zero, v)], axis=0)


def side_by_side(v):
    return jnp.concatenate([v[:T], v[T:]], axis=1)


def attend(q, k, v, allowed):
    s = nt(two_heads(q), k) * SCALE
    s = jnp.where(allowed, s, NEG)
    e = jnp.exp(s - jnp.max(s, axis=-1, keepdims=True))
    p = (e * (1.0 / jnp.sum(e, axis=-1, keepdims=True))).astype(BF)
    return p, nn(side_by_side(p), two_heads(v)).astype(BF)


def attend_back(q, k, v, p, dc):
    d2 = two_heads(dc)
    dp = nt(d2, v)
    dv = tn(p, d2).astype(BF)
    pf = p.astype(F32)
    ds = (pf * (dp - jnp.sum(pf * dp, axis=-1, keepdims=True))).astype(BF)
    dq = (nn(side_by_side(ds), two_heads(k)) * SCALE).astype(BF)
    dk = (tn(ds, two_heads(q)) * SCALE).astype(BF)
    return dq, dk, dv


def gelu_both(u):
    c = 0.7978845608028654
    u2 = u * u
    t = jnp.tanh(c * u * (1.0 + 0.044715 * u2))
    half = 0.5 * (1.0 + t)
    slope = half + 0.5 * u * (1.0 - t * t) * (c * (1.0 + 3.0 * 0.044715 * u2))
    return u * half, slope


def tile_at(i):
    return slice(i * T, (i + 1) * T)


SPANS = (128, 128, 64, 32)


def forward_rows(x_ref, g1, g2, wq, wk, wv, wo, n1, q, k, v, p, ctx, spans):
    xf = x_ref[...].astype(F32)
    n1[...] = (xf * inv_rms(xf) * g1[...].astype(F32)).astype(BF)
    for out, w in ((q, wq), (k, wk), (v, wv)):
        out[...] = nn(n1[...], w[...]).astype(BF)
    for i, span in enumerate(spans):
        allowed = causal(span)
        for j in range(PAIRS):
            at = (tile_at(i), tile_at(j))
            p[i, j], ctx[at] = attend(q[at], k[at], v[at], allowed)
    return xf, nn(ctx[...], wo[...])


def backward_rows(tiles, q, k, v, p, dctx, dq, dk, dv):
    for i in range(tiles):
        for j in range(PAIRS):
            at = (tile_at(i), tile_at(j))
            dq[at], dk[at], dv[at] = attend_back(q[at], k[at], v[at], p[i, j], dctx[at])


def pick_kernel(eighths, picks, tokens, cot, w_router, xr, cr, dm, mine_x, mine_d):
    s = lax.axis_index("seq")
    core = lax.axis_index("mlp") % 2
    eye = iota((T, T), 0) == iota((T, T), 1)
    for j in range(2):
        n = eighths[2 * s + j] * BLOCK
        col = jnp.sum(jnp.where(eye, picks[j : j + 1, :], 0), axis=1, keepdims=True)
        hot = (iota((T, 2 * T), 1) == col) & (iota((T, 2 * T), 0) < n)
        hot = jnp.where(hot, 1.0, 0.0).astype(BF)
        span = slice(2 * T * j, 2 * T * (j + 1))
        x = nn(hot, tokens[span, :])
        c = nn(hot, cot[span, :])
        gate = jnp.sum(x * w_router[...].astype(F32), axis=-1, keepdims=True)
        d = (gate.astype(BF).astype(F32) * c).astype(BF)
        xr[tile_at(j), :] = x.astype(BF)
        cr[tile_at(j), :] = c.astype(BF)
        dm[tile_at(j), :] = d

        @pl.when(core == j)
        def _():
            mine_x[...] = x.astype(BF)
            mine_d[...] = d


def own_kernel(
    xr, dm, g1, g2, wq, wk, wv, wo, wup, wdown,
    keep_n, keep_m, send_n, send_m, qc, kc, vc, pc, cc, ac,
    n1, q, k, v, p, ctx, att, n2, act, dup,
):
    core = lax.axis_index("mlp") % 2
    xf, attn = forward_rows(xr, g1, g2, wq, wk, wv, wo, n1, q, k, v, p, ctx, (T, T))
    att[...] = attn
    mid = xf + attn
    n2[...] = (mid * inv_rms(mid) * g2[...].astype(F32)).astype(BF)
    a, slope = gelu_both(nn(n2[...], wup[...]))
    act[...] = a.astype(BF)
    dup[...] = (slope * nt(dm[...], wdown[...])).astype(BF)
    dn = nt(dup[...], wup[...])
    mo = nn(act[...], wdown[...])
    for j in range(2):

        @pl.when(core == j)
        def _():
            keep_n[...] = dn[tile_at(j), :]
            keep_m[...] = mo[tile_at(j), :]
            send_n[...] = dn[tile_at(1 - j), :].astype(BF)
            send_m[...] = mo[tile_at(1 - j), :].astype(BF)
            for out, src in ((qc, q), (kc, k), (vc, v), (cc, ctx), (ac, att)):
                out[...] = src[tile_at(j), :]
            pc[...] = p[j]


def middle_kernel(dna, dnb, xr, cr, ac, g2, w_router, dattn, dmid_out, small):
    core = lax.axis_index("mlp") % 2
    rows = pl.ds(core * T, T)
    x = xr[rows, :].astype(F32)
    gate = jnp.sum(x * w_router[...].astype(F32), axis=-1, keepdims=True)
    gate = gate.astype(BF).astype(F32)
    mid = x + ac[...]
    r = inv_rms(mid)
    unit = mid * r
    dn = dna[...].astype(F32) + dnb[...].astype(F32)
    small[...] = jnp.sum(dn * unit, axis=0, keepdims=True)
    scaled = dn * g2[...].astype(F32)
    dmid = r * (scaled - unit * jnp.mean(scaled * unit, axis=-1, keepdims=True))
    dmid_out[...] = dmid
    dattn[...] = (gate * cr[rows, :].astype(F32) + dmid).astype(BF)


def own_back_kernel(
    dattn, dmid, small_in, moa, mob, xr, cr, ac, qc, kc, vc, pc, g1, w_router, wq, wk, wv, wo,
    res, small, dctx, dq, dk, dv,
):
    core = lax.axis_index("mlp") % 2
    rows = pl.ds(core * T, T)
    x = xr[rows, :].astype(F32)
    wr = w_router[...].astype(F32)
    gate = jnp.sum(x * wr, axis=-1, keepdims=True).astype(BF).astype(F32)
    branch = ac[...] + (moa[...].astype(F32) + mob[...].astype(F32))
    gg = jnp.sum(cr[rows, :].astype(F32) * branch, axis=-1, keepdims=True).astype(BF)
    res[:, :D] = (gate * branch).astype(BF)
    res[:, 2 * D :] = jnp.broadcast_to(gg, (T, T))
    dctx[...] = nt(dattn[...], wo[...]).astype(BF)
    for j in range(PAIRS):
        at = (slice(None), tile_at(j))
        dq[at], dk[at], dv[at] = attend_back(qc[at], kc[at], vc[at], pc[j], dctx[at])
    dn = nt(dq[...], wq[...]) + nt(dk[...], wk[...]) + nt(dv[...], wv[...])
    r = inv_rms(x)
    unit = x * r
    scaled = dn * g1[...].astype(F32)
    dx = r * (scaled - unit * jnp.mean(scaled * unit, axis=-1, keepdims=True))
    res[:, D : 2 * D] = (dmid[...] + dx).astype(BF)
    small[...] = jnp.zeros_like(small)
    small[0:1, :] = jnp.sum(gg.astype(F32) * x, axis=0, keepdims=True)
    small[1:2, :] = jnp.sum(dn * unit, axis=0, keepdims=True)
    small[2:3, :] = small_in[...]


def place_kernel(eighths, picks, tokens, cot, w_router, mine, other, mixed, grad):
    s = lax.axis_index("seq")
    core = lax.axis_index("mlp") % 2
    wr = w_router[...].astype(F32)
    for j in range(2):
        n = eighths[2 * s + j] * BLOCK
        span = slice(2 * T * j, 2 * T * (j + 1))
        hot = (iota((2 * T, T), 0) == picks[j : j + 1, :]) & (iota((2 * T, T), 1) < n)
        hot = jnp.where(hot, 1.0, 0.0).astype(BF)
        res = jnp.where(core == j, mine[...], other[...])
        out = nn(hot, res)
        mixed[span, :] = (tokens[span, :].astype(F32) + out[:, :D]).astype(BF)
        step = out[:, D : 2 * D] + out[:, 2 * D : 2 * D + 1] * wr
        grad[span, :] = (cot[span, :].astype(F32) + step).astype(BF)


def dense_kernel(eighths, own, r1, r2, r3, c1, c2, c3, dense, tile):
    s = lax.axis_index("seq")
    core = lax.axis_index("mlp") % 2
    pos = s % 4
    first = (s // 4) * GROUP
    size = [eighths[first + i] for i in range(GROUP)]
    start = []
    for i in range(GROUP):
        total = jnp.int32(0)
        for j in range(GROUP):
            ahead = (size[j] >= size[i]) if j < i else (size[j] > size[i])
            if j != i:
                total = total + jnp.where(ahead, size[j], 0)
        start.append(total)

    def of(values, at):
        out = values[0]
        for i in range(1, GROUP):
            out = jnp.where(at == i, values[i], out)
        return out

    def put(src, base, seq):
        count, to = of(size, seq), of(start, seq)
        for b in range(4):

            @pl.when(b < count)
            def _():
                dst = pl.multiple_of((to + b) * BLOCK, BLOCK)
                dense[pl.ds(dst, BLOCK), :] = src[base + b * BLOCK : base + (b + 1) * BLOCK, :]

    put(own, 0, 2 * pos)
    put(own, T, 2 * pos + 1)
    for step, mine, other in ((1, r1, c1), (2, r2, c2), (3, r3, c3)):
        put(mine, 0, 2 * (pos ^ step) + core)
        put(other, 0, 2 * (pos ^ step) + 1 - core)
    tile[...] = dense[pl.ds(pl.multiple_of((2 * (pos % 2) + core) * T, T), T), :]


def join_kernel(z, y, zc, yc, dense):
    pos = lax.axis_index("seq") % 2
    core = lax.axis_index("mlp") % 2
    for src, at in (
        (z, 2 * pos + core),
        (y, 2 * (1 - pos) + core),
        (zc, 2 * pos + 1 - core),
        (yc, 2 * (1 - pos) + 1 - core),
    ):
        dense[pl.ds(pl.multiple_of(at * T, T), T), :] = src[...]


def all_forward_kernel(x, g1, g2, wq, wk, wv, wo, n1, q, k, v, p, ctx, n2):
    xf, attn = forward_rows(x, g1, g2, wq, wk, wv, wo, n1, q, k, v, p, ctx, SPANS)
    mid = xf + attn
    n2[...] = (mid * inv_rms(mid) * g2[...].astype(F32)).astype(BF)


def all_mlp_kernel(n2, dm, wup, wdown, *rest):
    *before, gup, gdown, act, dup = rest
    a, slope = gelu_both(nn(n2[...], wup[...]))
    act[...] = a.astype(BF)
    dup[...] = (slope * nt(dm[...], wdown[...])).astype(BF)
    gup[...] = tn(n2[...], dup[...])
    gdown[...] = tn(act[...], dm[...])
    for out, old in zip((gup, gdown), before):
        out[...] = out[...] + old[...]


def all_back_kernel(dattn, n1, q, k, v, p, ctx, wo, *rest):
    *before, gq, gk, gv, go, dctx, dq, dk, dv = rest
    dctx[...] = nt(dattn[...], wo[...]).astype(BF)
    backward_rows(4, q, k, v, p, dctx, dq, dk, dv)
    for out, left, right in ((gq, n1, dq), (gk, n1, dk), (gv, n1, dv), (go, ctx, dattn)):
        out[...] = tn(left[...], right[...])
    for out, old in zip((gq, gk, gv, go), before):
        out[...] = out[...] + old[...]


VM = pl.BlockSpec(memory_space=pltpu.VMEM)
SM = pl.BlockSpec(memory_space=pltpu.SMEM)


def call(kernel, ins, outs, scratch=(), scalars=0, flops=0, limit=40):
    size = sum(a.size * a.dtype.itemsize for a in ins) + sum(
        functools.reduce(lambda a, b: a * b, s, 1) * jnp.dtype(t).itemsize for s, t in outs
    )
    return pl.pallas_call(
        kernel,
        out_shape=[jax.ShapeDtypeStruct(s, t) for s, t in outs],
        in_specs=[SM] * scalars + [VM] * (len(ins) - scalars),
        out_specs=[VM] * len(outs),
        scratch_shapes=[pltpu.VMEM(s, t) for s, t in scratch],
        compiler_params=pltpu.CompilerParams(vmem_limit_bytes=limit * MIB),
        cost_estimate=pl.CostEstimate(flops=flops, bytes_accessed=size, transcendentals=0),
    )(*ins)


def swap(value, axis, mask):
    pairs = [(i, i ^ mask) for i in range(lax.axis_size(axis))]
    return lax.ppermute(value, axis, pairs)


def near(mine):
    got = [swap(mine, "seq", k) for k in (1, 2, 3)]
    return got + [swap(g, "mlp", 1) for g in got]


def far(tile):
    z = swap(tile, "seq", 4)
    y = swap(z, "seq", 1)
    return z, y, swap(z, "mlp", 1), swap(y, "mlp", 1)


def local(
    tokens, cotangent, picks, eighths, w_router, gain_attn, gain_mlp,
    wq, wk, wv, wo, wup, wdown,
):
    wr, g1, g2 = (v.reshape(1, D) for v in (w_router, gain_attn, gain_mlp))
    unit = 2 * D * D

    def rows(n, t=BF):
        return ((n, D), t)

    def probs(n):
        return ((n, PAIRS, 2 * T, T), BF)

    xr, cr, dm, mine_x, mine_d = call(
        pick_kernel, (eighths, picks, tokens, cotangent, wr),
        [rows(2 * T)] * 3 + [rows(T)] * 2, scalars=1, flops=4 * T * 4 * T * D,
    )
    near_x = near(mine_x)
    keep_n, keep_m, send_n, send_m, qc, kc, vc, pc, cc, ac = call(
        own_kernel, (xr, dm, g1, g2, wq, wk, wv, wo, wup, wdown),
        [rows(T, F32)] * 2 + [rows(T)] * 5 + [((PAIRS, 2 * T, T), BF), rows(T), rows(T, F32)],
        [rows(2 * T)] * 4 + [probs(2), rows(2 * T), rows(2 * T, F32)] + [rows(2 * T)] * 3,
        flops=8 * 2 * T * unit,
    )
    near_d = near(mine_d)
    half_n = (keep_n + swap(send_n, "mlp", 1).astype(F32)).astype(BF)
    both_n = swap(half_n, "mlp", 2)
    half_m = (keep_m + swap(send_m, "mlp", 1).astype(F32)).astype(BF)
    both_m = swap(half_m, "mlp", 2)
    dattn, dmid, small = call(
        middle_kernel, (half_n, both_n, xr, cr, ac, g2, wr),
        [rows(T), rows(T, F32), ((1, D), F32)],
    )
    near_a = near(dattn)
    res, small = call(
        own_back_kernel,
        (dattn, dmid, small, half_m, both_m, xr, cr, ac, qc, kc, vc, pc, g1, wr, wq, wk, wv, wo),
        [((T, 2 * D + T), BF), rows(8, F32)], [rows(T)] * 4, flops=5 * T * unit,
    )
    other = swap(res, "mlp", 1)
    mixed, grad_tokens = call(
        place_kernel, (eighths, picks, tokens, cotangent, wr, res, other),
        [rows(4 * T)] * 2, scalars=1, flops=4 * T * T * 13 * T,
    )
    small = small + swap(small, "mlp", 1)
    mask = 1
    while mask < lax.axis_size("seq"):
        small = small + swap(small, "seq", mask)
        mask *= 2

    def dense(pair, got):
        return call(
            dense_kernel, (eighths, pair, *got), [rows(4 * T), rows(T)], scalars=1
        )

    def join(tile):
        return call(join_kernel, far(tile), [rows(4 * T)])[0]

    def all_forward(x):
        return call(
            all_forward_kernel, (x, g1, g2, wq, wk, wv, wo),
            [rows(4 * T)] * 4 + [probs(4)] + [rows(4 * T)] * 2, flops=6 * 4 * T * unit,
        )

    def all_mlp(n2, d, *before):
        return call(
            all_mlp_kernel, (n2, d, wup, wdown, *before), [rows(D, F32)] * 2,
            [rows(4 * T)] * 2, flops=4 * 4 * T * unit,
        )

    def all_back(da, saved, *before):
        return call(
            all_back_kernel, (da, *saved, wo, *before), [rows(D, F32)] * 4,
            [rows(4 * T)] * 4, flops=7 * 4 * T * unit, limit=50,
        )

    x_a, x_tile = dense(xr, near_x)
    *saved_a, n2_a = all_forward(x_a)
    d_a, d_tile = dense(dm, near_d)
    ups = all_mlp(n2_a, d_a)
    *saved_b, n2_b = all_forward(join(x_tile))
    dattn_pair = [dattn, swap(dattn, "mlp", 1)]
    core = lax.axis_index("mlp") % 2
    pair = jnp.where(core == 0, jnp.concatenate(dattn_pair), jnp.concatenate(dattn_pair[::-1]))
    a_a, a_tile = dense(pair, near_a)
    grads = all_back(a_a, saved_a)
    gup, gdown = all_mlp(n2_b, join(d_tile), *ups)
    gq, gk, gv, go = all_back(join(a_tile), saved_b, *grads)
    total = (gq, gk, gv, go, gup, gdown)
    mask = 8
    while mask < lax.axis_size("seq"):
        total = [g + swap(g, "seq", mask) for g in total]
        mask *= 2
    return (mixed, grad_tokens, small[0], small[1], small[2], *total)


def solution(mesh):
    rows, cols, split, full = P("seq", None), P(None, "mlp"), P("mlp", None), P()
    return jax.shard_map(
        local,
        mesh=mesh,
        in_specs=(rows, rows, rows) + (full,) * 8 + (cols, split),
        out_specs=(rows, rows) + (full,) * 7 + (cols, split),
        check_vma=False,
    )
```

```python
import jax
import jax.numpy as jnp
from jax import lax
from jax.experimental import pallas as pl
from jax.experimental.pallas import tpu as pltpu
from jax.sharding import PartitionSpec as P

F32 = jnp.float32
BF = jnp.bfloat16
EPS = 1e-06
NEG = -1e30
SCALE = 0.125
D = 768
T = 128
PAIRS = 6
GROUP = 8
BLOCK = 32
MIB = 2**20


def nn(a, b):
    return lax.dot_general(a, b, (((1,), (0,)), ((), ())), preferred_element_type=F32)


def nt(a, b):
    return lax.dot_general(a, b, (((1,), (1,)), ((), ())), preferred_element_type=F32)


def tn(a, b):
    return lax.dot_general(a, b, (((0,), (0,)), ((), ())), preferred_element_type=F32)


def iota(shape, dim):
    return lax.broadcasted_iota(jnp.int32, shape, dim)


def row(ref):
    return ref[...].astype(F32).reshape(1, D)


def inv_rms(v):
    return lax.rsqrt(jnp.mean(v * v, axis=-1, keepdims=True) + EPS)


def causal(span):
    keys, queries = iota((T, 2 * T), 0), iota((T, 2 * T), 1) % T
    return (keys <= queries) & (keys // span == queries // span)


def first_head():
    return iota((T, T), 1) < 64


def two_heads(v):
    zero = jnp.zeros((), BF)
    low = first_head()
    return jnp.concatenate([jnp.where(low, v, zero), jnp.where(low, zero, v)], axis=0)


def one_pair(v):
    return jnp.where(first_head(), v[:T], v[T:])


def stagger(count, stages):
    for n in range(count + len(stages) - 1):
        for s, stage in enumerate(stages):
            if 0 <= n - s < count:
                stage(n - s, (n - s) % 4)


def place_of(n):
    return n // PAIRS, n % PAIRS, (tile_at(n // PAIRS), tile_at(n % PAIRS))


def attend(q, k, v, p, ctx, spans, raw):
    def score(n, slot):
        i, j, at = place_of(n)
        raw[slot] = nt(k[at], two_heads(q[at]))

    def softmax(n, slot):
        i, j, at = place_of(n)
        s = jnp.where(causal(spans[i]), raw[slot] * SCALE, NEG)
        e = jnp.exp(s - jnp.max(s, axis=0, keepdims=True))
        p[i, j] = (e * (1.0 / jnp.sum(e, axis=0, keepdims=True))).astype(BF)

    def mix(n, slot):
        i, j, at = place_of(n)
        ctx[at] = one_pair(tn(p[i, j], v[at])).astype(BF)

    stagger(len(spans) * PAIRS, (score, softmax, mix))


def attend_back(tiles, q, k, v, p, dctx, dq, dk, dv, wide, raw, ds):
    def score(n, slot):
        i, j, at = place_of(n)
        wide[slot] = two_heads(dctx[at])
        raw[slot] = nt(v[at], wide[slot])

    def softmax(n, slot):
        i, j, at = place_of(n)
        pf, dp = p[i, j].astype(F32), raw[slot]
        ds[slot] = (pf * (dp - jnp.sum(pf * dp, axis=0, keepdims=True))).astype(BF)
        dv[at] = nn(p[i, j], wide[slot]).astype(BF)

    def mix(n, slot):
        i, j, at = place_of(n)
        dk[at] = (nn(ds[slot], two_heads(q[at])) * SCALE).astype(BF)
        dq[at] = (one_pair(tn(ds[slot], k[at])) * SCALE).astype(BF)

    stagger(tiles * PAIRS, (score, softmax, mix))


FORE = [((4, T, 2 * T), F32)]
BACK = [((4, 2 * T, T), BF), ((4, T, 2 * T), F32), ((4, T, 2 * T), BF)]


def gelu_both(u):
    c = 0.7978845608028654
    u2 = u * u
    t = jnp.tanh(c * u * (1.0 + 0.044715 * u2))
    half = 0.5 * (1.0 + t)
    slope = half + 0.5 * u * (1.0 - t * t) * (c * (1.0 + 3.0 * 0.044715 * u2))
    return u * half, slope


def tile_at(i):
    return slice(i * T, (i + 1) * T)


SPANS = (128, 128, 64, 32)


def forward_rows(x_ref, g1, wq, wk, wv, wo, n1, q, k, v, p, ctx, spans, raw, ready):
    xf = x_ref[...].astype(F32)
    n1[...] = (xf * inv_rms(xf) * row(g1)).astype(BF)
    for i, (out, w) in enumerate(((q, wq), (k, wk), (v, wv))):
        ready(i)
        out[...] = nn(n1[...], w[...]).astype(BF)
    attend(q, k, v, p, ctx, spans, raw)
    ready(3)
    return xf, nn(ctx[...], wo[...])


def pick_kernel(
    h_eighths, h_picks, h_tokens, h_cot, h_router,
    xr, cr, dm, mine_x, mine_d, other_x, other_d,
    eighths, picks, tokens, cot, w_router, sem,
):
    pairs = (
        (h_eighths, eighths), (h_picks, picks), (h_tokens, tokens),
        (h_router, w_router), (h_cot, cot),
    )
    loads = [pltpu.make_async_copy(h, v, sem.at[i]) for i, (h, v) in enumerate(pairs)]
    for load in loads:
        load.start()
    for load in loads:
        load.wait()
    s = lax.axis_index("seq")
    core = lax.axis_index("mlp") % 2
    eye = iota((T, T), 0) == iota((T, T), 1)
    for j in range(2):
        n = eighths[2 * s + j] * BLOCK
        col = jnp.sum(jnp.where(eye, picks[j : j + 1, :], 0), axis=1, keepdims=True)
        hot = (iota((T, 2 * T), 1) == col) & (iota((T, 2 * T), 0) < n)
        hot = jnp.where(hot, 1.0, 0.0).astype(BF)
        span = slice(2 * T * j, 2 * T * (j + 1))
        x = nn(hot, tokens[span, :])
        c = nn(hot, cot[span, :])
        gate = jnp.sum(x * row(w_router), axis=-1, keepdims=True)
        d = (gate.astype(BF).astype(F32) * c).astype(BF)
        xr[tile_at(j), :] = x.astype(BF)
        cr[tile_at(j), :] = c.astype(BF)
        dm[tile_at(j), :] = d

        @pl.when(core == j)
        def _():
            mine_x[:T, :] = x.astype(BF)
            mine_d[...] = d

        @pl.when(core != j)
        def _():
            other_x[...] = x.astype(BF)
            other_d[...] = d


def own_kernel(
    xr, dm, hg1, hg2, hq, hk, hv, ho, hup, hdown,
    keep_n, keep_m, send_n, send_m, qc, kc, vc, pc, ac,
    n1, q, k, v, p, ctx, att, n2, act, dup, raw, g1, g2, wq, wk, wv, wo, wup, wdown, sem,
):
    core = lax.axis_index("mlp") % 2
    pairs = ((hq, wq), (hk, wk), (hv, wv), (ho, wo), (hup, wup), (hdown, wdown), (hg1, g1), (hg2, g2))
    loads = [pltpu.make_async_copy(h, w, sem.at[i]) for i, (h, w) in enumerate(pairs)]
    for i in (6, 0, 1, 2, 7):
        loads[i].start()
    loads[6].wait()

    def ready(i):
        loads[i].wait()
        if i == 0:
            for j in (3, 4, 5):
                loads[j].start()

    xf, attn = forward_rows(xr, g1, wq, wk, wv, wo, n1, q, k, v, p, ctx, (T, T), raw, ready)
    loads[7].wait()
    att[...] = attn
    mid = xf + attn
    n2[...] = (mid * inv_rms(mid) * row(g2)).astype(BF)
    loads[4].wait()
    a, slope = gelu_both(nn(n2[...], wup[...]))
    act[...] = a.astype(BF)
    loads[5].wait()
    dup[...] = (slope * nt(dm[...], wdown[...])).astype(BF)
    dn = nt(dup[...], wup[...])
    mo = nn(act[...], wdown[...])
    for j in range(2):

        @pl.when(core == j)
        def _():
            keep_n[...] = dn[tile_at(j), :]
            keep_m[...] = mo[tile_at(j), :]
            send_n[...] = dn[tile_at(1 - j), :].astype(BF)
            send_m[...] = mo[tile_at(1 - j), :].astype(BF)
            for out, src in ((qc, q), (kc, k), (vc, v), (ac, att)):
                out[...] = src[tile_at(j), :]
            pc[0] = p[j]


def middle_kernel(dna, dnb, xr, cr, ac, g2, w_router, dattn, dmid_out, small):
    core = lax.axis_index("mlp") % 2
    rows = pl.ds(core * T, T)
    x = xr[rows, :].astype(F32)
    gate = jnp.sum(x * row(w_router), axis=-1, keepdims=True)
    gate = gate.astype(BF).astype(F32)
    mid = x + ac[...]
    r = inv_rms(mid)
    unit = mid * r
    dn = dna[...].astype(F32) + dnb[...].astype(F32)
    small[...] = jnp.sum(dn * unit, axis=0, keepdims=True)
    scaled = dn * row(g2)
    dmid = r * (scaled - unit * jnp.mean(scaled * unit, axis=-1, keepdims=True))
    dmid_out[...] = dmid
    dattn[:T, :] = (gate * cr[rows, :].astype(F32) + dmid).astype(BF)


def own_back_kernel(
    dattn, dmid, small_in, moa, mob, xr, cr, ac, qc, kc, vc, pc, g1, w_router, wq, wk, wv, wo,
    res, dctx, dq, dk, dv, *work,
):
    core = lax.axis_index("mlp") % 2
    rows = pl.ds(core * T, T)
    x = xr[rows, :].astype(F32)
    wr = row(w_router)
    gate = jnp.sum(x * wr, axis=-1, keepdims=True).astype(BF).astype(F32)
    branch = ac[...] + (moa[...].astype(F32) + mob[...].astype(F32))
    gg = jnp.sum(cr[rows, :].astype(F32) * branch, axis=-1, keepdims=True).astype(BF)
    res[:T, :D] = (gate * branch).astype(BF)
    res[:T, 2 * D :] = jnp.broadcast_to(gg, (T, T))
    dctx[...] = nt(dattn[:T, :], wo[...]).astype(BF)
    attend_back(1, qc, kc, vc, pc, dctx, dq, dk, dv, *work)
    dn = nt(dq[...], wq[...]) + nt(dk[...], wk[...]) + nt(dv[...], wv[...])
    r = inv_rms(x)
    unit = x * r
    scaled = dn * row(g1)
    dx = r * (scaled - unit * jnp.mean(scaled * unit, axis=-1, keepdims=True))
    res[:T, D : 2 * D] = (dmid[...] + dx).astype(BF)
    total = jnp.concatenate(
        [
            jnp.sum(gg.astype(F32) * x, axis=0, keepdims=True),
            jnp.sum(dn * unit, axis=0, keepdims=True),
            small_in[...],
            jnp.zeros((13, D), F32),
        ],
        axis=0,
    )
    high = total.astype(BF)
    res[T : T + 16, :D] = high
    res[T : T + 16, D : 2 * D] = (total - high.astype(F32)).astype(BF)
    res[T : T + 16, 2 * D :] = jnp.zeros((16, T), BF)


def place_kernel(
    eighths, picks, w_router, mine, other, h_tokens, h_cot,
    h_mixed, h_grad, tokens, cot, mixed, grad, sem,
):
    s = lax.axis_index("seq")
    core = lax.axis_index("mlp") % 2
    wr = row(w_router)
    spans = [slice(2 * T * j, 2 * T * (j + 1)) for j in range(2)]
    loads = [
        [
            pltpu.make_async_copy(h.at[spans[j]], v.at[spans[j]], sem.at[2 * j + i])
            for i, (h, v) in enumerate(((h_tokens, tokens), (h_cot, cot)))
        ]
        for j in range(2)
    ]
    for load in loads[0] + loads[1]:
        load.start()
    stores = []
    for j, span in enumerate(spans):
        n = eighths[2 * s + j] * BLOCK
        hot = (iota((2 * T, T), 0) == picks[j : j + 1, :]) & (iota((2 * T, T), 1) < n)
        hot = jnp.where(hot, 1.0, 0.0).astype(BF)
        res = jnp.where(core == j, mine[:T, :], other[:T, :])
        out = nn(hot, res)
        for load in loads[j]:
            load.wait()
        mixed[span, :] = (tokens[span, :].astype(F32) + out[:, :D]).astype(BF)
        step = out[:, D : 2 * D] + out[:, 2 * D : 2 * D + 1] * wr
        grad[span, :] = (cot[span, :].astype(F32) + step).astype(BF)
        for i, (v, h) in enumerate(((mixed, h_mixed), (grad, h_grad))):
            stores.append(pltpu.make_async_copy(v.at[span], h.at[span], sem.at[4 + 2 * j + i]))
            stores[-1].start()
    for store in stores:
        store.wait()


def dense_kernel(eighths, *refs):
    same, cross, dense, tile = refs[:4], refs[4:8], refs[8], refs[9]
    s = lax.axis_index("seq")
    core = lax.axis_index("mlp") % 2
    pos = s % 4
    first = (s // 4) * GROUP
    size = [eighths[first + i] for i in range(GROUP)]
    start = []
    for i in range(GROUP):
        total = jnp.int32(0)
        for j in range(GROUP):
            ahead = (size[j] >= size[i]) if j < i else (size[j] > size[i])
            if j != i:
                total = total + jnp.where(ahead, size[j], 0)
        start.append(total)

    def of(values, at):
        out = values[0]
        for i in range(1, GROUP):
            out = jnp.where(at == i, values[i], out)
        return out

    def put(src, seq):
        count, to = of(size, seq), of(start, seq)
        for b in range(4):

            @pl.when(b < count)
            def _():
                dst = pl.multiple_of((to + b) * BLOCK, BLOCK)
                dense[pl.ds(dst, BLOCK), :] = src[b * BLOCK : (b + 1) * BLOCK, :]

    for i in range(4):
        put(same[i], 2 * (pos ^ i) + core)
        put(cross[i], 2 * (pos ^ i) + 1 - core)
    tile[:T, :] = dense[pl.ds(pl.multiple_of((2 * (pos % 2) + core) * T, T), T), :]


def relay_kernel(*refs):
    n = len(refs) // 2
    for src, out in zip(refs[:n], refs[n:]):
        out[:T, :] = src[:T, :]


def join_kernel(z, y, zc, yc, dense):
    pos = lax.axis_index("seq") % 2
    core = lax.axis_index("mlp") % 2
    for half, same, cross in ((pos, z, zc), (1 - pos, y, yc)):
        for src, at in ((same, 2 * half + core), (cross, 2 * half + 1 - core)):
            dense[pl.ds(pl.multiple_of(at * T, T), T), :] = src[...]


def all_forward_kernel(x, g1, g2, wq, wk, wv, wo, n1, q, k, v, p, ctx, n2, raw):
    xf, attn = forward_rows(x, g1, wq, wk, wv, wo, n1, q, k, v, p, ctx, SPANS, raw, lambda i: None)
    mid = xf + attn
    n2[...] = (mid * inv_rms(mid) * row(g2)).astype(BF)


def grad_out(outs, bufs, tmp, sem, parts):
    step, stores = D // 3, []
    for i, (left, right, more_left, more_right) in enumerate(parts):
        for j in range(3):
            at = slice(j * step, (j + 1) * step)
            bufs[i][at, :] = tn(left[:, at], right[...])
            tmp[j][...] = tn(more_left[:, at], more_right[...])
            bufs[i][at, :] = bufs[i][at, :] + tmp[j][...]
            stores.append(pltpu.make_async_copy(bufs[i].at[at], outs[i].at[at], sem.at[3 * i + j]))
            stores[-1].start()
    for store in stores:
        store.wait()


def mlp_rows(n2, dm, wup, wdown, act, dup):
    a, slope = gelu_both(nn(n2[...], wup[...]))
    act[...] = a.astype(BF)
    dup[...] = (slope * nt(dm[...], wdown[...])).astype(BF)


def all_mlp_kernel(n2, dm, wup, wdown, act, dup):
    mlp_rows(n2, dm, wup, wdown, act, dup)


def last_mlp_kernel(
    n2, dm, wup, wdown, n2_a, dm_a, act_a, dup_a, gup, gdown, act, dup, b0, b1, t0, t1, t2, sem
):
    mlp_rows(n2, dm, wup, wdown, act, dup)
    parts = ((act, dm, act_a, dm_a), (n2, dup, n2_a, dup_a))
    grad_out((gdown, gup), (b0, b1), (t0, t1, t2), sem, parts)


def all_back_kernel(dattn, q, k, v, p, wo, dq, dk, dv, dctx, *work):
    dctx[...] = nt(dattn[...], wo[...]).astype(BF)
    attend_back(4, q, k, v, p, dctx, dq, dk, dv, *work)


def last_back_kernel(
    dattn, q, k, v, p, wo, n1, ctx, dattn_a, n1_a, ctx_a, dq_a, dk_a, dv_a,
    gq, gk, gv, go, dq, dk, dv, dctx, w0, w1, w2, b0, b1, b2, b3, t0, t1, t2, sem,
):
    all_back_kernel(dattn, q, k, v, p, wo, dq, dk, dv, dctx, w0, w1, w2)
    parts = (
        (ctx, dattn, ctx_a, dattn_a),
        (n1, dv, n1_a, dv_a),
        (n1, dk, n1_a, dk_a),
        (n1, dq, n1_a, dq_a),
    )
    grad_out((go, gv, gk, gq), (b0, b1, b2, b3), (t0, t1, t2), sem, parts)


def fold_both_kernel(keep_n, keep_m, came_n, came_m, half_n, half_m):
    half_n[...] = (keep_n[...] + came_n[...].astype(F32)).astype(BF)
    half_m[...] = (keep_m[...] + came_m[...].astype(F32)).astype(BF)


def fold_kernel(a, b, out):
    out[...] = a[...] + b[...]


def unpack_kernel(mine, other, out):
    def whole(ref):
        rows = ref[T : T + 16, :].astype(F32)
        return rows[:8, :D] + rows[:8, D : 2 * D]

    out[...] = whole(mine) + whole(other)


def last_fold_kernel(a, b, o0, o1, o2):
    v = a[...] + b[...]
    for i, out in enumerate((o0, o1, o2)):
        out[...] = v[i]


LIMIT = {
    "pick_kernel": 8, "own_kernel": 24, "middle_kernel": 8, "own_back_kernel": 16,
    "place_kernel": 10, "dense_kernel": 8, "join_kernel": 6, "all_forward_kernel": 20,
    "all_mlp_kernel": 12, "last_mlp_kernel": 20, "all_back_kernel": 10, "last_back_kernel": 26,
    "fold_both_kernel": 4, "fold_kernel": 4, "unpack_kernel": 4, "last_fold_kernel": 4,
    "relay_kernel": 4,
}


VM = pl.BlockSpec(memory_space=pltpu.VMEM)
SM = pl.BlockSpec(memory_space=pltpu.SMEM)
HB = pl.BlockSpec(memory_space=pltpu.HBM)
AN = pl.BlockSpec(memory_space=pl.ANY)


def call(
    kernel, ins, outs, scratch=(), scalars=0, after=(), through=(), hbm_in=0, hbm_out=False,
    sems=0,
):
    n, skip, name, m, t = len(ins), len(after), kernel.__name__, len(outs), len(through)

    def body(*refs):
        given, made = refs[n + skip : n + skip + t], refs[n + skip + t + m :][:t]
        for old, new in zip(given, made):
            new[...] = old[...]
        kernel(*refs[:n], *refs[n + skip + t :][:m], *refs[n + skip + t + m + t :])

    own = n - scalars - hbm_in
    return pl.pallas_call(
        body,
        name=name,
        out_shape=[jax.ShapeDtypeStruct(s, d) for s, d in outs]
        + [jax.ShapeDtypeStruct(v.shape, v.dtype) for v in through],
        in_specs=[SM] * scalars + [VM] * own + [HB] * hbm_in + [AN] * skip + [VM] * t,
        out_specs=[HB if hbm_out else VM] * m + [VM] * t,
        scratch_shapes=[like(v) for v in scratch]
        + ([pltpu.SemaphoreType.DMA((sems,))] if sems else []),
        compiler_params=pltpu.CompilerParams(vmem_limit_bytes=LIMIT[name] * MIB),
        cost_estimate=pl.CostEstimate(flops=1000, bytes_accessed=1000, transcendentals=0),
    )(*ins, *after, *through)


def like(v):
    if isinstance(v, tuple):
        return pltpu.VMEM(*v)
    return (pltpu.SMEM if v.dtype == jnp.int32 and v.ndim == 1 else pltpu.VMEM)(v.shape, v.dtype)


def far_off(v):
    return pltpu.with_memory_space_constraint(v, pltpu.HBM)


def swap(value, axis, mask):
    pairs = [(i, i ^ mask) for i in range(lax.axis_size(axis))]
    return lax.ppermute(value, axis, pairs)


def rows(n, t=BF):
    return ((n, D), t)


def probs(n):
    return ((n, PAIRS, T, 2 * T), BF)


def local(
    tokens, cotangent, picks, eighths, w_router, gain_attn, gain_mlp,
    wq, wk, wv, wo, wup, wdown,
):
    wr, g1, g2 = w_router, gain_attn, gain_mlp

    def relay(parts, after=(), pads=None):
        sizes = [rows(T + 8 * p) for p in pads or [0] * len(parts)]
        return call(relay_kernel, parts, sizes, after=after)

    def dense(same, cross, after=(), through=(), pad=0):
        return call(
            dense_kernel, (eighths, *same, *cross), [rows(4 * T), rows(T + 8 * pad)], scalars=1,
            after=after, through=through,
        )

    def join(parts, after=()):
        return call(join_kernel, parts, [rows(4 * T)], after=after)[0]

    def core(v):
        return swap(v, "mlp", 1)

    def all_forward(x, after=(), through=()):
        return call(
            all_forward_kernel, (x, g1, g2, wq, wk, wv, wo),
            [rows(4 * T)] * 4 + [probs(4)] + [rows(4 * T)] * 2, FORE, after=after, through=through,
        )

    def fold(v, mask, after=()):
        return call(fold_kernel, (v, swap(v, "seq", mask)), [rows(8, F32)], after=after)[0]

    xr, cr, dm, mine_x, mine_d, other_x, other_d = call(
        pick_kernel, [far_off(v) for v in (eighths, picks, tokens, cotangent, wr)],
        [rows(2 * T)] * 3 + [rows(T + 16)] + [rows(T)] * 3,
        [eighths, picks, rows(4 * T), rows(4 * T), wr], hbm_in=5, sems=5,
    )
    x1, x2 = swap(mine_x, "seq", 1), swap(mine_x, "seq", 2)
    keep_n, keep_m, send_n, send_m, qc, kc, vc, pc, ac = call(
        own_kernel, (xr, dm, *(far_off(v) for v in (g1, g2, wq, wk, wv, wo, wup, wdown))),
        [rows(T, F32)] * 2 + [rows(T)] * 5 + [probs(1), rows(T, F32)],
        [rows(2 * T)] * 4 + [probs(2), rows(2 * T), rows(2 * T, F32)] + [rows(2 * T)] * 3
        + FORE + [g1, g2] + [rows(D)] * 6, hbm_in=8, sems=8,
    )
    half_n, half_m = call(
        fold_both_kernel, (keep_n, keep_m, core(send_n), core(send_m)), [rows(T)] * 2
    )
    both_n = swap(half_n, "mlp", 2)
    x0, x1, x2, mine_d = relay([mine_x, x1, x2, mine_d], after=(half_n,))
    x3, c1, c2 = swap(x1, "seq", 2), core(x1), core(x2)
    d1 = swap(mine_d, "seq", 1)
    dattn, dmid, small = call(
        middle_kernel, (half_n, both_n, xr, cr, ac, g2, wr),
        [rows(T + 16), rows(T, F32), ((1, D), F32)], after=(x1,),
    )
    a1, a2, a3 = [swap(dattn, "seq", k) for k in (1, 2, 3)]
    x3, c1, c2 = relay([x3, c1, c2], after=(dattn,))
    c3 = core(x3)
    x_a, x_tile, half_m, mine_d = dense(
        (x0, x1, x2, x3), (other_x, c1, c2, c3), through=(half_m, mine_d), pad=1
    )
    far_x = swap(x_tile, "seq", 4)
    both_m = swap(half_m, "mlp", 2)
    n1_a, q_a, k_a, v_a, p_a, ctx_a, n2_a = all_forward(x_a)
    same_a = relay([dattn, a1, a2, a3], after=(n2_a,))
    cross_a = [core(v) for v in same_a]
    (res,) = call(
        own_back_kernel,
        (dattn, dmid, small, half_m, both_m, xr, cr, ac, qc, kc, vc, pc, g1, wr, wq, wk, wv, wo),
        [((T + 16, 2 * D + T), BF)], [rows(T)] * 4 + BACK, after=(same_a[0],),
    )
    a_a, a_tile = dense(same_a, cross_a, after=(res,), pad=1)
    far_a = swap(a_tile, "seq", 4)
    (far_x,) = relay([far_x], after=(a_a,))
    near_x, cross_x = swap(far_x, "seq", 1), core(far_x)
    d1, d0 = relay([d1, mine_d], after=(far_x,))
    d2, d3, e1 = swap(d0, "seq", 2), swap(d1, "seq", 2), core(d1)
    dq_a, dk_a, dv_a, res = call(
        all_back_kernel, (a_a, q_a, k_a, v_a, p_a, wo), [rows(4 * T)] * 3,
        [rows(4 * T)] + BACK, after=(d1,), through=(res,),
    )
    other = core(res)
    d2, d3, e1 = relay([d2, d3, e1], after=(dq_a,))
    e2, e3 = core(d2), core(d3)
    mixed, grad_tokens = call(
        place_kernel, (eighths, picks, wr, res, other, far_off(tokens), far_off(cotangent)),
        [rows(4 * T)] * 2, [rows(4 * T)] * 4, scalars=1, hbm_in=2, hbm_out=True, sems=8,
        after=(d2,),
    )
    d_a, d_tile = dense((d0, d1, d2, d3), (other_d, e1, e2, e3), after=(mixed,))
    far_d = swap(d_tile, "seq", 4)
    (small,) = call(unpack_kernel, (res, other), [rows(8, F32)], after=(d_a,))
    act_a, dup_a = call(
        all_mlp_kernel, (n2_a, d_a, wup, wdown), [rows(4 * T)] * 2, after=(small,)
    )
    small = fold(small, 1, after=(act_a,))
    (far_a,) = relay([far_a], after=(small,))
    near_a, cross_a = swap(far_a, "seq", 1), core(far_a)
    near_x, cross_x = relay([near_x, cross_x], after=(far_a,))
    next_x = core(near_x)
    n1_b, q_b, k_b, v_b, p_b, ctx_b, n2_b = all_forward(join((far_x, near_x, cross_x, next_x)))
    small = fold(small, 2, after=(n2_b,))
    near_a, cross_a = relay([near_a, cross_a], after=(small,))
    next_a = core(near_a)
    (far_d,) = relay([far_d], after=(near_a,))
    near_d, cross_d = swap(far_d, "seq", 1), core(far_d)
    a_b = join((far_a, near_a, cross_a, next_a), after=(far_d,))
    gq, gk, gv, go = call(
        last_back_kernel,
        (a_b, q_b, k_b, v_b, p_b, wo, n1_b, ctx_b, a_a, n1_a, ctx_a, dq_a, dk_a, dv_a),
        [rows(D, F32)] * 4,
        [rows(4 * T)] * 4 + BACK + [rows(D, F32)] * 4 + [rows(D // 3, F32)] * 3,
        hbm_out=True, sems=12,
    )
    near_d, cross_d = relay([near_d, cross_d], after=(gq,))
    next_d = core(near_d)
    mask = 4
    while mask < lax.axis_size("seq") // 2:
        small = fold(small, mask)
        mask *= 2
    smalls = call(
        last_fold_kernel, (small, swap(small, "seq", mask)), [((D,), F32)] * 3, after=(near_d,)
    )
    d_b = join((far_d, near_d, cross_d, next_d), after=(smalls[0],))
    gup, gdown = call(
        last_mlp_kernel, (n2_b, d_b, wup, wdown, n2_a, d_a, act_a, dup_a),
        [rows(D, F32)] * 2,
        [rows(4 * T)] * 2 + [rows(D, F32)] * 2 + [rows(D // 3, F32)] * 3,
        hbm_out=True, sems=6,
    )
    total = [gq, gk, gv, go, gup, gdown]
    mask = 8
    while mask < lax.axis_size("seq"):
        total = [g + swap(g, "seq", mask) for g in total]
        mask *= 2
    return (mixed, grad_tokens, *smalls, *total)


def solution(mesh):
    rows, cols, split, full = P("seq", None), P(None, "mlp"), P("mlp", None), P()
    return jax.shard_map(
        local,
        mesh=mesh,
        in_specs=(rows, rows, rows) + (full,) * 8 + (cols, split),
        out_specs=(rows, rows) + (full,) * 7 + (cols, split),
        check_vma=False,
    )
```

```python
import functools

import jax
import jax.numpy as jnp
from jax import lax
from jax.experimental import pallas as pl
from jax.experimental.pallas import tpu as pltpu
from jax.sharding import PartitionSpec as P

F32 = jnp.float32
BF = jnp.bfloat16
EPS = 1e-06
NEG = -1e30
SCALE = 0.125
D = 768
T = 128
PAIRS = 6
GROUP = 8
BLOCK = 32
MIB = 2**20
XD = 16


def nn(a, b):
    return lax.dot_general(a, b, (((1,), (0,)), ((), ())), preferred_element_type=F32)


def nt(a, b):
    return lax.dot_general(a, b, (((1,), (1,)), ((), ())), preferred_element_type=F32)


def tn(a, b):
    return lax.dot_general(a, b, (((0,), (0,)), ((), ())), preferred_element_type=F32)


def iota(shape, dim):
    return lax.broadcasted_iota(jnp.int32, shape, dim)


def row(ref):
    return ref[...].astype(F32).reshape(1, D)


def inv_rms(v):
    return lax.rsqrt(jnp.mean(v * v, axis=-1, keepdims=True) + EPS)


def causal(span):
    keys, queries = iota((T, 2 * T), 0), iota((T, 2 * T), 1) % T
    return (keys <= queries) & (keys // span == queries // span)


def first_head():
    return iota((T, T), 1) < 64


def two_heads(v):
    zero = jnp.zeros((), BF)
    low = first_head()
    return jnp.concatenate([jnp.where(low, v, zero), jnp.where(low, zero, v)], axis=0)


def one_pair(v):
    return jnp.where(first_head(), v[:T], v[T:])


def stagger(count, stages):
    for n in range(count + len(stages) - 1):
        for s, stage in enumerate(stages):
            if 0 <= n - s < count:
                stage(n - s, (n - s) % 4)


def place_of(n):
    return n // PAIRS, n % PAIRS, (tile_at(n // PAIRS), tile_at(n % PAIRS))


def attend(q, k, v, p, ctx, spans, raw):
    def score(n, slot):
        i, j, at = place_of(n)
        raw[slot] = nt(k[at], two_heads(q[at]))

    def softmax(n, slot):
        i, j, at = place_of(n)
        s = jnp.where(causal(spans[i]), raw[slot] * SCALE, NEG)
        e = jnp.exp(s - jnp.max(s, axis=0, keepdims=True))
        p[i, j] = (e * (1.0 / jnp.sum(e, axis=0, keepdims=True))).astype(BF)

    def mix(n, slot):
        i, j, at = place_of(n)
        ctx[at] = one_pair(tn(p[i, j], v[at])).astype(BF)

    stagger(len(spans) * PAIRS, (score, softmax, mix))


def attend_back(tiles, q, k, v, p, dctx, dq, dk, dv, wide, raw, ds):
    def score(n, slot):
        i, j, at = place_of(n)
        wide[slot] = two_heads(dctx[at])
        raw[slot] = nt(v[at], wide[slot])

    def softmax(n, slot):
        i, j, at = place_of(n)
        pf, dp = p[i, j].astype(F32), raw[slot]
        ds[slot] = (pf * (dp - jnp.sum(pf * dp, axis=0, keepdims=True))).astype(BF)
        dv[at] = nn(p[i, j], wide[slot]).astype(BF)

    def mix(n, slot):
        i, j, at = place_of(n)
        dk[at] = (nn(ds[slot], two_heads(q[at])) * SCALE).astype(BF)
        dq[at] = (one_pair(tn(ds[slot], k[at])) * SCALE).astype(BF)

    stagger(tiles * PAIRS, (score, softmax, mix))


FORE = [((4, T, 2 * T), F32)]
BACK = [((4, 2 * T, T), BF), ((4, T, 2 * T), F32), ((4, T, 2 * T), BF)]


def gelu_both(u):
    c = 0.7978845608028654
    u2 = u * u
    t = jnp.tanh(c * u * (1.0 + 0.044715 * u2))
    half = 0.5 * (1.0 + t)
    slope = half + 0.5 * u * (1.0 - t * t) * (c * (1.0 + 3.0 * 0.044715 * u2))
    return u * half, slope


def tile_at(i):
    return slice(i * T, (i + 1) * T)


SPANS = (128, 128, 64, 32)


def forward_rows(x_ref, g1, wq, wk, wv, wo, n1, q, k, v, p, ctx, spans, raw, ready):
    xf = x_ref[...].astype(F32)
    n1[...] = (xf * inv_rms(xf) * row(g1)).astype(BF)
    for i, (out, w) in enumerate(((q, wq), (k, wk), (v, wv))):
        ready(i)
        out[...] = nn(n1[...], w[...]).astype(BF)
    attend(q, k, v, p, ctx, spans, raw)
    ready(3)
    return xf, nn(ctx[...], wo[...])


def pick_kernel(
    h_eighths, h_picks, h_tokens, h_cot, h_router,
    xr, cr, dm, mine, other,
    eighths, picks, tokens, cot, w_router, sem,
):
    pairs = (
        (h_eighths, eighths), (h_picks, picks), (h_tokens, tokens),
        (h_router, w_router), (h_cot, cot),
    )
    loads = [pltpu.make_async_copy(h, v, sem.at[i]) for i, (h, v) in enumerate(pairs)]
    for load in loads:
        load.start()
    for load in loads:
        load.wait()
    s = lax.axis_index("seq")
    core = lax.axis_index("mlp") % 2
    eye = iota((T, T), 0) == iota((T, T), 1)
    for j in range(2):
        n = eighths[2 * s + j] * BLOCK
        col = jnp.sum(jnp.where(eye, picks[j : j + 1, :], 0), axis=1, keepdims=True)
        hot = (iota((T, 2 * T), 1) == col) & (iota((T, 2 * T), 0) < n)
        hot = jnp.where(hot, 1.0, 0.0).astype(BF)
        span = slice(2 * T * j, 2 * T * (j + 1))
        x = nn(hot, tokens[span, :])
        c = nn(hot, cot[span, :])
        gate = jnp.sum(x * row(w_router), axis=-1, keepdims=True)
        d = (gate.astype(BF).astype(F32) * c).astype(BF)
        xr[tile_at(j), :] = x.astype(BF)
        cr[tile_at(j), :] = c.astype(BF)
        dm[tile_at(j), :] = d

        for out, own in ((mine, core == j), (other, core != j)):

            @pl.when(own)
            def _():
                out[:T, :] = x.astype(BF)
                out[T : 2 * T, :] = d


def own_kernel(
    xr, dm, hg1, hg2, hq, hk, hv, ho, hup, hdown,
    keep_n, keep_m, send_n, send_m, qc, kc, vc, pc, ac,
    n1, q, k, v, p, ctx, att, n2, act, dup, raw, g1, g2, wq, wk, wv, wo, wup, wdown, sem,
):
    core = lax.axis_index("mlp") % 2
    pairs = ((hq, wq), (hk, wk), (hv, wv), (ho, wo), (hup, wup), (hdown, wdown), (hg1, g1), (hg2, g2))
    loads = [pltpu.make_async_copy(h, w, sem.at[i]) for i, (h, w) in enumerate(pairs)]
    for i in (6, 0, 1, 2, 7):
        loads[i].start()
    loads[6].wait()

    def ready(i):
        loads[i].wait()
        if i == 0:
            for j in (3, 4, 5):
                loads[j].start()

    xf, attn = forward_rows(xr, g1, wq, wk, wv, wo, n1, q, k, v, p, ctx, (T, T), raw, ready)
    loads[7].wait()
    att[...] = attn
    mid = xf + attn
    n2[...] = (mid * inv_rms(mid) * row(g2)).astype(BF)
    loads[4].wait()
    a, slope = gelu_both(nn(n2[...], wup[...]))
    act[...] = a.astype(BF)
    loads[5].wait()
    dup[...] = (slope * nt(dm[...], wdown[...])).astype(BF)
    dn = nt(dup[...], wup[...])
    mo = nn(act[...], wdown[...])
    for j in range(2):

        @pl.when(core == j)
        def _():
            keep_n[...] = dn[tile_at(j), :]
            keep_m[...] = mo[tile_at(j), :]
            send_n[...] = dn[tile_at(1 - j), :].astype(BF)
            send_m[...] = mo[tile_at(1 - j), :].astype(BF)
            for out, src in ((qc, q), (kc, k), (vc, v), (ac, att)):
                out[...] = src[tile_at(j), :]
            pc[0] = p[j]


def middle_kernel(dna, dnb, xr, cr, ac, g2, w_router, dattn, dmid_out, small):
    core = lax.axis_index("mlp") % 2
    rows = pl.ds(core * T, T)
    x = xr[rows, :].astype(F32)
    gate = jnp.sum(x * row(w_router), axis=-1, keepdims=True)
    gate = gate.astype(BF).astype(F32)
    mid = x + ac[...]
    r = inv_rms(mid)
    unit = mid * r
    dn = dna[...].astype(F32) + dnb[...].astype(F32)
    small[...] = jnp.sum(dn * unit, axis=0, keepdims=True)
    scaled = dn * row(g2)
    dmid = r * (scaled - unit * jnp.mean(scaled * unit, axis=-1, keepdims=True))
    dmid_out[...] = dmid
    dattn[:T, :] = (gate * cr[rows, :].astype(F32) + dmid).astype(BF)


def own_back_kernel(
    dattn, dmid, small_in, moa, mob, xr, cr, ac, qc, kc, vc, pc, g1, w_router, wq, wk, wv, wo,
    delta, back, misc, dctx, dq, dk, dv, *work,
):
    core = lax.axis_index("mlp") % 2
    rows = pl.ds(core * T, T)
    x = xr[rows, :].astype(F32)
    wr = row(w_router)
    gate = jnp.sum(x * wr, axis=-1, keepdims=True).astype(BF).astype(F32)
    branch = ac[...] + (moa[...].astype(F32) + mob[...].astype(F32))
    gg = jnp.sum(cr[rows, :].astype(F32) * branch, axis=-1, keepdims=True).astype(BF)
    delta[...] = (gate * branch).astype(BF)
    dctx[...] = nt(dattn[:T, :], wo[...]).astype(BF)
    attend_back(1, qc, kc, vc, pc, dctx, dq, dk, dv, *work)
    dn = nt(dq[...], wq[...]) + nt(dk[...], wk[...]) + nt(dv[...], wv[...])
    r = inv_rms(x)
    unit = x * r
    scaled = dn * row(g1)
    dx = r * (scaled - unit * jnp.mean(scaled * unit, axis=-1, keepdims=True))
    back[...] = (dmid[...] + dx).astype(BF)
    eye = iota((T, T), 0) == iota((T, T), 1)
    across = jnp.sum(jnp.where(eye, gg.astype(F32), 0.0), axis=0, keepdims=True)
    total = jnp.concatenate(
        [
            jnp.sum(gg.astype(F32) * x, axis=0, keepdims=True),
            jnp.sum(dn * unit, axis=0, keepdims=True),
            small_in[...],
            jnp.concatenate([across, jnp.zeros((1, D - T), F32)], axis=1),
            jnp.zeros((12, D), F32),
        ],
        axis=0,
    )
    high = total.astype(BF)
    misc[:16, :] = high
    misc[16:, :] = (total - high.astype(F32)).astype(BF)


def place_kernel(
    eighths, picks, w_router, delta, back, misc, delta_o, back_o, misc_o, h_tokens, h_cot,
    h_mixed, h_grad, tokens, cot, mixed, grad, sem,
):
    s = lax.axis_index("seq")
    core = lax.axis_index("mlp") % 2
    wr = row(w_router)
    spans = [slice(2 * T * j, 2 * T * (j + 1)) for j in range(2)]
    loads = [
        [
            pltpu.make_async_copy(h.at[spans[j]], v.at[spans[j]], sem.at[2 * j + i])
            for i, (h, v) in enumerate(((h_tokens, tokens), (h_cot, cot)))
        ]
        for j in range(2)
    ]
    for load in loads[0] + loads[1]:
        load.start()
    stores = []
    eye = iota((T, T), 0) == iota((T, T), 1)
    for j, span in enumerate(spans):
        n = eighths[2 * s + j] * BLOCK
        hot = (iota((2 * T, T), 0) == picks[j : j + 1, :]) & (iota((2 * T, T), 1) < n)
        hot = jnp.where(hot, 1.0, 0.0).astype(BF)
        mine = core == j
        gg = jnp.where(mine, misc[3:4, :T], misc_o[3:4, :T]).astype(F32)
        gg = jnp.sum(jnp.where(eye, gg, 0.0), axis=1, keepdims=True)
        gg = nn(hot, jnp.broadcast_to(gg, (T, T)).astype(BF))[:, :1]
        forth = nn(hot, jnp.where(mine, delta[...], delta_o[...]))
        down = nn(hot, jnp.where(mine, back[...], back_o[...]))
        for load in loads[j]:
            load.wait()
        mixed[span, :] = (tokens[span, :].astype(F32) + forth).astype(BF)
        grad[span, :] = (cot[span, :].astype(F32) + (down + gg * wr)).astype(BF)
        for i, (v, h) in enumerate(((mixed, h_mixed), (grad, h_grad))):
            stores.append(pltpu.make_async_copy(v.at[span], h.at[span], sem.at[4 + 2 * j + i]))
            stores[-1].start()
    for store in stores:
        store.wait()


def dense_kernel(base, eighths, *refs):
    same, cross, dense, tile = refs[:4], refs[4:8], refs[8], refs[9]
    s = lax.axis_index("seq")
    core = lax.axis_index("mlp") % 2
    pos = s % 4
    first = (s // 4) * GROUP
    size = [eighths[first + i] for i in range(GROUP)]
    start = []
    for i in range(GROUP):
        total = jnp.int32(0)
        for j in range(GROUP):
            ahead = (size[j] >= size[i]) if j < i else (size[j] > size[i])
            if j != i:
                total = total + jnp.where(ahead, size[j], 0)
        start.append(total)

    def of(values, at):
        out = values[0]
        for i in range(1, GROUP):
            out = jnp.where(at == i, values[i], out)
        return out

    def put(src, seq):
        count, to = of(size, seq), of(start, seq)
        for b in range(4):

            @pl.when(b < count)
            def _():
                dst = pl.multiple_of((to + b) * BLOCK, BLOCK)
                dense[pl.ds(dst, BLOCK), :] = src[base + b * BLOCK : base + (b + 1) * BLOCK, :]

    for i in range(4):
        put(same[i], 2 * (pos ^ i) + core)
        put(cross[i], 2 * (pos ^ i) + 1 - core)
    tile[:T, :] = dense[pl.ds(pl.multiple_of((2 * (pos % 2) + core) * T, T), T), :]


def relay_kernel(*refs):
    n = len(refs) // 2
    for src, out in zip(refs[:n], refs[n:]):
        size = min(src.shape[0], out.shape[0]) // T * T
        out[:size, :] = src[:size, :]


def join_kernel(z, y, zc, yc, dense):
    pos = lax.axis_index("seq") % 2
    core = lax.axis_index("mlp") % 2
    for half, same, cross in ((pos, z, zc), (1 - pos, y, yc)):
        for src, at in ((same, 2 * half + core), (cross, 2 * half + 1 - core)):
            dense[pl.ds(pl.multiple_of(at * T, T), T), :] = src[...]


def all_forward_kernel(x, g1, g2, wq, wk, wv, wo, n1, q, k, v, p, ctx, n2, raw):
    xf, attn = forward_rows(x, g1, wq, wk, wv, wo, n1, q, k, v, p, ctx, SPANS, raw, lambda i: None)
    mid = xf + attn
    n2[...] = (mid * inv_rms(mid) * row(g2)).astype(BF)


def grad_out(outs, bufs, tmp, sem, parts):
    step, stores = D // 3, []
    for i, (left, right, more_left, more_right) in enumerate(parts):
        for j in range(3):
            at = slice(j * step, (j + 1) * step)
            bufs[i][at, :] = tn(left[:, at], right[...])
            tmp[j][...] = tn(more_left[:, at], more_right[...])
            bufs[i][at, :] = bufs[i][at, :] + tmp[j][...]
            stores.append(pltpu.make_async_copy(bufs[i].at[at], outs[i].at[at], sem.at[3 * i + j]))
            stores[-1].start()
    for store in stores:
        store.wait()


def mlp_rows(n2, dm, wup, wdown, act, dup):
    a, slope = gelu_both(nn(n2[...], wup[...]))
    act[...] = a.astype(BF)
    dup[...] = (slope * nt(dm[...], wdown[...])).astype(BF)


def all_mlp_kernel(n2, dm, wup, wdown, act, dup):
    mlp_rows(n2, dm, wup, wdown, act, dup)


def last_mlp_kernel(
    n2, dm, wup, wdown, n2_a, dm_a, act_a, dup_a, gup, gdown, act, dup, b0, b1, t0, t1, t2, sem
):
    mlp_rows(n2, dm, wup, wdown, act, dup)
    parts = ((act, dm, act_a, dm_a), (n2, dup, n2_a, dup_a))
    grad_out((gdown, gup), (b0, b1), (t0, t1, t2), sem, parts)


def all_back_kernel(dattn, q, k, v, p, wo, dq, dk, dv, dctx, *work):
    dctx[...] = nt(dattn[...], wo[...]).astype(BF)
    attend_back(4, q, k, v, p, dctx, dq, dk, dv, *work)


def last_back_kernel(
    dattn, q, k, v, p, wo, n1, ctx, dattn_a, n1_a, ctx_a, dq_a, dk_a, dv_a,
    gq, gk, gv, go, dq, dk, dv, dctx, w0, w1, w2, b0, b1, b2, b3, t0, t1, t2, sem,
):
    all_back_kernel(dattn, q, k, v, p, wo, dq, dk, dv, dctx, w0, w1, w2)
    parts = (
        (ctx, dattn, ctx_a, dattn_a),
        (n1, dv, n1_a, dv_a),
        (n1, dk, n1_a, dk_a),
        (n1, dq, n1_a, dq_a),
    )
    grad_out((go, gv, gk, gq), (b0, b1, b2, b3), (t0, t1, t2), sem, parts)


def fold_both_kernel(keep_n, keep_m, came_n, came_m, half_n, half_m):
    half_n[...] = (keep_n[...] + came_n[...].astype(F32)).astype(BF)
    half_m[...] = (keep_m[...] + came_m[...].astype(F32)).astype(BF)


def fold_kernel(a, b, out):
    out[...] = a[...] + b[...]


def unpack_kernel(mine, other, out):
    def whole(ref):
        return ref[:8, :].astype(F32) + ref[16:24, :].astype(F32)

    out[...] = whole(mine) + whole(other)


def last_fold_kernel(a, b, o0, o1, o2):
    v = a[...] + b[...]
    for i, out in enumerate((o0, o1, o2)):
        out[...] = v[i]


LIMIT = {
    "pick_kernel": 8, "own_kernel": 24, "middle_kernel": 8, "own_back_kernel": 16,
    "place_kernel": 10, "dense_kernel": 8, "join_kernel": 6, "all_forward_kernel": 20,
    "all_mlp_kernel": 12, "last_mlp_kernel": 20, "all_back_kernel": 10, "last_back_kernel": 26,
    "fold_both_kernel": 4, "fold_kernel": 4, "unpack_kernel": 4, "last_fold_kernel": 4,
    "relay_kernel": 4,
}


VM = pl.BlockSpec(memory_space=pltpu.VMEM)
SM = pl.BlockSpec(memory_space=pltpu.SMEM)
HB = pl.BlockSpec(memory_space=pltpu.HBM)
AN = pl.BlockSpec(memory_space=pl.ANY)


def call(
    kernel, ins, outs, scratch=(), scalars=0, after=(), through=(), hbm_in=0, hbm_out=False,
    sems=0,
):
    n, skip, m, t = len(ins), len(after), len(outs), len(through)
    name = getattr(kernel, "func", kernel).__name__

    def body(*refs):
        given, made = refs[n + skip : n + skip + t], refs[n + skip + t + m :][:t]
        for old, new in zip(given, made):
            new[...] = old[...]
        kernel(*refs[:n], *refs[n + skip + t :][:m], *refs[n + skip + t + m + t :])

    own = n - scalars - hbm_in
    return pl.pallas_call(
        body,
        name=name,
        out_shape=[jax.ShapeDtypeStruct(s, d) for s, d in outs]
        + [jax.ShapeDtypeStruct(v.shape, v.dtype) for v in through],
        in_specs=[SM] * scalars + [VM] * own + [HB] * hbm_in + [AN] * skip + [VM] * t,
        out_specs=[HB if hbm_out else VM] * m + [VM] * t,
        scratch_shapes=[like(v) for v in scratch]
        + ([pltpu.SemaphoreType.DMA((sems,))] if sems else []),
        compiler_params=pltpu.CompilerParams(vmem_limit_bytes=LIMIT[name] * MIB),
        cost_estimate=pl.CostEstimate(flops=1000, bytes_accessed=1000, transcendentals=0),
    )(*ins, *after, *through)


def like(v):
    if isinstance(v, tuple):
        return pltpu.VMEM(*v)
    return (pltpu.SMEM if v.dtype == jnp.int32 and v.ndim == 1 else pltpu.VMEM)(v.shape, v.dtype)


def far_off(v):
    return pltpu.with_memory_space_constraint(v, pltpu.HBM)


def swap(value, axis, mask):
    pairs = [(i, i ^ mask) for i in range(lax.axis_size(axis))]
    return lax.ppermute(value, axis, pairs)


def rows(n, t=BF):
    return ((n, D), t)


def probs(n):
    return ((n, PAIRS, T, 2 * T), BF)


def local(
    tokens, cotangent, picks, eighths, w_router, gain_attn, gain_mlp,
    wq, wk, wv, wo, wup, wdown,
):
    wr, g1, g2 = w_router, gain_attn, gain_mlp

    def relay(parts, after=(), through=()):
        sizes = [rows(v.shape[0] // T * T) for v in parts]
        return call(relay_kernel, parts, sizes, after=after)

    def dense(same, cross, base=0, after=(), through=(), pad=0):
        return call(
            functools.partial(dense_kernel, base), (eighths, *same, *cross),
            [rows(4 * T), rows(T + 8 * pad)], scalars=1, after=after, through=through,
        )

    def join(parts, after=()):
        return call(join_kernel, parts, [rows(4 * T)], after=after)[0]

    def core(v):
        return swap(v, "mlp", 1)

    def all_forward(x, after=(), through=()):
        return call(
            all_forward_kernel, (x, g1, g2, wq, wk, wv, wo),
            [rows(4 * T)] * 4 + [probs(4)] + [rows(4 * T)] * 2, FORE, after=after, through=through,
        )

    def fold(v, mask, after=()):
        return call(fold_kernel, (v, swap(v, "seq", mask)), [rows(8, F32)], after=after)[0]

    xr, cr, dm, mine, other = call(
        pick_kernel, [far_off(v) for v in (eighths, picks, tokens, cotangent, wr)],
        [rows(2 * T)] * 3 + [rows(2 * T + XD)] + [rows(2 * T)],
        [eighths, picks, rows(4 * T), rows(4 * T), wr], hbm_in=5, sems=5,
    )
    near = [swap(mine, "seq", k) for k in (1, 2, 3)]
    keep_n, keep_m, send_n, send_m, qc, kc, vc, pc, ac = call(
        own_kernel, (xr, dm, *(far_off(v) for v in (g1, g2, wq, wk, wv, wo, wup, wdown))),
        [rows(T, F32)] * 2 + [rows(T)] * 5 + [probs(1), rows(T, F32)],
        [rows(2 * T)] * 4 + [probs(2), rows(2 * T), rows(2 * T, F32)] + [rows(2 * T)] * 3
        + FORE + [g1, g2] + [rows(D)] * 6, hbm_in=8, sems=8,
    )
    half_n, half_m = call(
        fold_both_kernel, (keep_n, keep_m, core(send_n), core(send_m)), [rows(T)] * 2
    )
    both_n = swap(half_n, "mlp", 2)
    dattn, dmid, small, half_m = call(
        middle_kernel, (half_n, both_n, xr, cr, ac, g2, wr),
        [rows(T + 16), rows(T, F32), ((1, D), F32)], through=(half_m,),
    )
    a1, a2, a3 = [swap(dattn, "seq", k) for k in (1, 2, 3)]
    both_m = swap(half_m, "mlp", 2)
    near = relay(near, after=(dattn,))
    same, cross = (mine, *near), (other, *(core(v) for v in near))
    x_a, x_tile = dense(same, cross, pad=2)
    far_x = swap(x_tile, "seq", 4)
    n1_a, q_a, k_a, v_a, p_a, ctx_a, n2_a = all_forward(x_a)
    same_a = relay([dattn, a1, a2, a3], after=(n2_a,))
    cross_a = [core(v) for v in same_a]
    res = call(
        own_back_kernel,
        (dattn, dmid, small, half_m, both_m, xr, cr, ac, qc, kc, vc, pc, g1, wr, wq, wk, wv, wo),
        [rows(T), rows(T), rows(32)], [rows(T)] * 4 + BACK, after=(same_a[0],),
    )
    a_a, a_tile = dense(same_a, cross_a, after=(res[0],), pad=1)
    far_a = swap(a_tile, "seq", 4)
    d_a, d_tile = dense(same, cross, base=T, after=(a_a,))
    (far_x,) = relay([far_x], after=(d_a,))
    near_x, cross_x = swap(far_x, "seq", 1), core(far_x)
    dq_a, dk_a, dv_a, *res = call(
        all_back_kernel, (a_a, q_a, k_a, v_a, p_a, wo), [rows(4 * T)] * 3,
        [rows(4 * T)] + BACK, after=(far_x,), through=res,
    )
    other = [core(v) for v in res]
    act_a, dup_a = call(
        all_mlp_kernel, (n2_a, d_a, wup, wdown), [rows(4 * T)] * 2, after=(dq_a,)
    )
    mixed, grad_tokens, d_tile = call(
        place_kernel, (eighths, picks, wr, *res, *other, far_off(tokens), far_off(cotangent)),
        [rows(4 * T)] * 2, [rows(4 * T)] * 4, scalars=1, hbm_in=2, hbm_out=True, sems=8,
        after=(act_a,), through=(d_tile,),
    )
    far_d = swap(d_tile, "seq", 4)
    (small,) = call(unpack_kernel, (res[2], other[2]), [rows(8, F32)], after=(d_tile,))
    near_x, cross_x = relay([near_x, cross_x], after=(small,))
    next_x = core(near_x)
    (far_a,) = relay([far_a], after=(near_x,))
    near_a, cross_a = swap(far_a, "seq", 1), core(far_a)
    n1_b, q_b, k_b, v_b, p_b, ctx_b, n2_b = all_forward(
        join((far_x, near_x, cross_x, next_x), after=(far_a,))
    )
    small = fold(small, 1, after=(n2_b,))
    near_a, cross_a = relay([near_a, cross_a], after=(small,))
    next_a = core(near_a)
    (far_d,) = relay([far_d], after=(near_a,))
    near_d, cross_d = swap(far_d, "seq", 1), core(far_d)
    a_b = join((far_a, near_a, cross_a, next_a), after=(far_d,))
    gq, gk, gv, go, token = call(
        last_back_kernel,
        (a_b, q_b, k_b, v_b, p_b, wo, n1_b, ctx_b, a_a, n1_a, ctx_a, dq_a, dk_a, dv_a),
        [rows(D, F32)] * 4,
        [rows(4 * T)] * 4 + BACK + [rows(D, F32)] * 4 + [rows(D // 3, F32)] * 3,
        hbm_out=True, sems=12, through=(small,),
    )
    small = fold(small, 2, after=(token,))
    near_d, cross_d = relay([near_d, cross_d], after=(small,))
    d_b = join((far_d, near_d, cross_d, core(near_d)))
    gup, gdown, token = call(
        last_mlp_kernel, (n2_b, d_b, wup, wdown, n2_a, d_a, act_a, dup_a),
        [rows(D, F32)] * 2,
        [rows(4 * T)] * 2 + [rows(D, F32)] * 2 + [rows(D // 3, F32)] * 3,
        hbm_out=True, sems=6, through=(small,),
    )
    mask = 4
    while mask < lax.axis_size("seq") // 2:
        small = fold(small, mask)
        mask *= 2
    smalls = call(
        last_fold_kernel, (small, swap(small, "seq", mask)), [((D,), F32)] * 3, after=(token,)
    )
    total = [gq, gk, gv, go, gup, gdown]
    mask = 8
    while mask < lax.axis_size("seq"):
        total = [g + swap(g, "seq", mask) for g in total]
        mask *= 2
    return (mixed, grad_tokens, *smalls, *total)


def solution(mesh):
    rows, cols, split, full = P("seq", None), P(None, "mlp"), P("mlp", None), P()
    return jax.shard_map(
        local,
        mesh=mesh,
        in_specs=(rows, rows, rows) + (full,) * 8 + (cols, split),
        out_specs=(rows, rows) + (full,) * 7 + (cols, split),
        check_vma=False,
    )
```

```python
import functools

import jax
import jax.numpy as jnp
from jax import lax
from jax.experimental import pallas as pl
from jax.experimental.pallas import tpu as pltpu
from jax.sharding import PartitionSpec as P

F32 = jnp.float32
BF = jnp.bfloat16
EPS = 1e-06
NEG = -1e30
SCALE = 0.125
D = 768
T = 128
PAIRS = 6
GROUP = 8
BLOCK = 32
MIB = 2**20
XD = 16


def nn(a, b):
    return lax.dot_general(a, b, (((1,), (0,)), ((), ())), preferred_element_type=F32)


def nt(a, b):
    return lax.dot_general(a, b, (((1,), (1,)), ((), ())), preferred_element_type=F32)


def tn(a, b):
    return lax.dot_general(a, b, (((0,), (0,)), ((), ())), preferred_element_type=F32)


def iota(shape, dim):
    return lax.broadcasted_iota(jnp.int32, shape, dim)


def row(ref):
    return ref[...].astype(F32).reshape(1, D)


def inv_rms(v):
    return lax.rsqrt(jnp.mean(v * v, axis=-1, keepdims=True) + EPS)


def causal(span):
    keys, queries = iota((T, 2 * T), 0), iota((T, 2 * T), 1) % T
    return (keys <= queries) & (keys // span == queries // span)


def first_head():
    return iota((T, T), 1) < 64


def two_heads(v):
    zero = jnp.zeros((), BF)
    low = first_head()
    return jnp.concatenate([jnp.where(low, v, zero), jnp.where(low, zero, v)], axis=0)


def one_pair(v):
    return jnp.where(first_head(), v[:T], v[T:])


def stagger(count, stages):
    for n in range(count + len(stages) - 1):
        for s, stage in enumerate(stages):
            if 0 <= n - s < count:
                stage(n - s, (n - s) % 4)


def place_of(n):
    return n // PAIRS, n % PAIRS, (tile_at(n // PAIRS), tile_at(n % PAIRS))


def attend(q, k, v, p, ctx, spans, raw):
    def score(n, slot):
        i, j, at = place_of(n)
        raw[slot] = nt(k[at], two_heads(q[at]))

    def softmax(n, slot):
        i, j, at = place_of(n)
        s = jnp.where(causal(spans[i]), raw[slot] * SCALE, NEG)
        e = jnp.exp(s - jnp.max(s, axis=0, keepdims=True))
        p[i, j] = (e * (1.0 / jnp.sum(e, axis=0, keepdims=True))).astype(BF)

    def mix(n, slot):
        i, j, at = place_of(n)
        ctx[at] = one_pair(tn(p[i, j], v[at])).astype(BF)

    stagger(len(spans) * PAIRS, (score, softmax, mix))


def attend_back(tiles, q, k, v, p, dctx, dq, dk, dv, wide, raw, ds):
    def score(n, slot):
        i, j, at = place_of(n)
        wide[slot] = two_heads(dctx[at])
        raw[slot] = nt(v[at], wide[slot])

    def softmax(n, slot):
        i, j, at = place_of(n)
        pf, dp = p[i, j].astype(F32), raw[slot]
        ds[slot] = (pf * (dp - jnp.sum(pf * dp, axis=0, keepdims=True))).astype(BF)
        dv[at] = nn(p[i, j], wide[slot]).astype(BF)

    def mix(n, slot):
        i, j, at = place_of(n)
        dk[at] = (nn(ds[slot], two_heads(q[at])) * SCALE).astype(BF)
        dq[at] = (one_pair(tn(ds[slot], k[at])) * SCALE).astype(BF)

    stagger(tiles * PAIRS, (score, softmax, mix))


FORE = [((4, T, 2 * T), F32)]
BACK = [((4, 2 * T, T), BF), ((4, T, 2 * T), F32), ((4, T, 2 * T), BF)]


def gelu_both(u):
    c = 0.7978845608028654
    u2 = u * u
    t = jnp.tanh(c * u * (1.0 + 0.044715 * u2))
    half = 0.5 * (1.0 + t)
    slope = half + 0.5 * u * (1.0 - t * t) * (c * (1.0 + 3.0 * 0.044715 * u2))
    return u * half, slope


def tile_at(i):
    return slice(i * T, (i + 1) * T)


SPANS = (128, 128, 64, 32)


def forward_rows(x_ref, g1, wq, wk, wv, wo, n1, q, k, v, p, ctx, spans, raw, ready):
    xf = x_ref[...].astype(F32)
    n1[...] = (xf * inv_rms(xf) * row(g1)).astype(BF)
    for i, (out, w) in enumerate(((q, wq), (k, wk), (v, wv))):
        ready(i)
        out[...] = nn(n1[...], w[...]).astype(BF)
    attend(q, k, v, p, ctx, spans, raw)
    ready(3)
    return xf, nn(ctx[...], wo[...])


def pick_kernel(
    h_eighths, h_picks, h_tokens, h_cot, h_router,
    xr, cr, dm, mine, other, tokens, cot,
    eighths, picks, w_router, sem,
):
    pairs = (
        (h_eighths, eighths), (h_picks, picks), (h_tokens, tokens),
        (h_router, w_router), (h_cot, cot),
    )
    loads = [pltpu.make_async_copy(h, v, sem.at[i]) for i, (h, v) in enumerate(pairs)]
    for load in loads:
        load.start()
    for load in loads:
        load.wait()
    s = lax.axis_index("seq")
    core = lax.axis_index("mlp") % 2
    eye = iota((T, T), 0) == iota((T, T), 1)
    for j in range(2):
        n = eighths[2 * s + j] * BLOCK
        col = jnp.sum(jnp.where(eye, picks[j : j + 1, :], 0), axis=1, keepdims=True)
        hot = (iota((T, 2 * T), 1) == col) & (iota((T, 2 * T), 0) < n)
        hot = jnp.where(hot, 1.0, 0.0).astype(BF)
        span = slice(2 * T * j, 2 * T * (j + 1))
        x = nn(hot, tokens[span, :])
        c = nn(hot, cot[span, :])
        gate = jnp.sum(x * row(w_router), axis=-1, keepdims=True)
        d = (gate.astype(BF).astype(F32) * c).astype(BF)
        xr[tile_at(j), :] = x.astype(BF)
        cr[tile_at(j), :] = c.astype(BF)
        dm[tile_at(j), :] = d

        for out, own in ((mine, core == j), (other, core != j)):

            @pl.when(own)
            def _():
                out[:T, :] = x.astype(BF)
                out[T : 2 * T, :] = d


def own_kernel(
    xr, dm, hg1, hg2, hq, hk, hv, ho, hup, hdown,
    keep_n, keep_m, send_n, send_m, qc, kc, vc, pc, ac,
    n1, q, k, v, p, ctx, att, n2, act, dup, raw, g1, g2, wq, wk, wv, wo, wup, wdown, sem,
):
    core = lax.axis_index("mlp") % 2
    pairs = ((hq, wq), (hk, wk), (hv, wv), (ho, wo), (hup, wup), (hdown, wdown), (hg1, g1), (hg2, g2))
    loads = [pltpu.make_async_copy(h, w, sem.at[i]) for i, (h, w) in enumerate(pairs)]
    for i in (6, 0, 1, 2, 7):
        loads[i].start()
    loads[6].wait()

    def ready(i):
        loads[i].wait()
        if i == 0:
            for j in (3, 4, 5):
                loads[j].start()

    xf, attn = forward_rows(xr, g1, wq, wk, wv, wo, n1, q, k, v, p, ctx, (T, T), raw, ready)
    loads[7].wait()
    att[...] = attn
    mid = xf + attn
    n2[...] = (mid * inv_rms(mid) * row(g2)).astype(BF)
    loads[4].wait()
    a, slope = gelu_both(nn(n2[...], wup[...]))
    act[...] = a.astype(BF)
    loads[5].wait()
    dup[...] = (slope * nt(dm[...], wdown[...])).astype(BF)
    dn = nt(dup[...], wup[...])
    mo = nn(act[...], wdown[...])
    for j in range(2):

        @pl.when(core == j)
        def _():
            keep_n[...] = dn[tile_at(j), :]
            keep_m[...] = mo[tile_at(j), :]
            send_n[...] = dn[tile_at(1 - j), :].astype(BF)
            send_m[...] = mo[tile_at(1 - j), :].astype(BF)
            for out, src in ((qc, q), (kc, k), (vc, v), (ac, att)):
                out[...] = src[tile_at(j), :]
            pc[0] = p[j]


def middle_kernel(dna, dnb, xr, cr, ac, g2, w_router, dattn, dmid_out, small):
    core = lax.axis_index("mlp") % 2
    rows = pl.ds(core * T, T)
    x = xr[rows, :].astype(F32)
    gate = jnp.sum(x * row(w_router), axis=-1, keepdims=True)
    gate = gate.astype(BF).astype(F32)
    mid = x + ac[...]
    r = inv_rms(mid)
    unit = mid * r
    dn = dna[...].astype(F32) + dnb[...].astype(F32)
    small[...] = jnp.sum(dn * unit, axis=0, keepdims=True)
    scaled = dn * row(g2)
    dmid = r * (scaled - unit * jnp.mean(scaled * unit, axis=-1, keepdims=True))
    dmid_out[...] = dmid
    dattn[:T, :] = (gate * cr[rows, :].astype(F32) + dmid).astype(BF)


def own_back_kernel(
    dattn, dmid, small_in, moa, mob, xr, cr, ac, qc, kc, vc, pc, g1, w_router, wq, wk, wv, wo,
    delta, back, misc, dctx, dq, dk, dv, *work,
):
    core = lax.axis_index("mlp") % 2
    rows = pl.ds(core * T, T)
    x = xr[rows, :].astype(F32)
    wr = row(w_router)
    gate = jnp.sum(x * wr, axis=-1, keepdims=True).astype(BF).astype(F32)
    branch = ac[...] + (moa[...].astype(F32) + mob[...].astype(F32))
    gg = jnp.sum(cr[rows, :].astype(F32) * branch, axis=-1, keepdims=True).astype(BF)
    delta[...] = (gate * branch).astype(BF)
    dctx[...] = nt(dattn[:T, :], wo[...]).astype(BF)
    attend_back(1, qc, kc, vc, pc, dctx, dq, dk, dv, *work)
    dn = nt(dq[...], wq[...]) + nt(dk[...], wk[...]) + nt(dv[...], wv[...])
    r = inv_rms(x)
    unit = x * r
    scaled = dn * row(g1)
    dx = r * (scaled - unit * jnp.mean(scaled * unit, axis=-1, keepdims=True))
    back[...] = (dmid[...] + dx).astype(BF)
    eye = iota((T, T), 0) == iota((T, T), 1)
    across = jnp.sum(jnp.where(eye, gg.astype(F32), 0.0), axis=0, keepdims=True)
    total = jnp.concatenate(
        [
            jnp.sum(gg.astype(F32) * x, axis=0, keepdims=True),
            jnp.sum(dn * unit, axis=0, keepdims=True),
            small_in[...],
            jnp.concatenate([across, jnp.zeros((1, D - T), F32)], axis=1),
            jnp.zeros((12, D), F32),
        ],
        axis=0,
    )
    high = total.astype(BF)
    misc[:16, :] = high
    misc[16:, :] = (total - high.astype(F32)).astype(BF)


def place_kernel(
    eighths, picks, w_router, delta, back, misc, delta_o, back_o, misc_o, tokens, cot,
    h_mixed, h_grad, mixed, grad, sem,
):
    s = lax.axis_index("seq")
    core = lax.axis_index("mlp") % 2
    wr = row(w_router)
    spans = [slice(2 * T * j, 2 * T * (j + 1)) for j in range(2)]
    stores = []
    eye = iota((T, T), 0) == iota((T, T), 1)
    for j, span in enumerate(spans):
        n = eighths[2 * s + j] * BLOCK
        hot = (iota((2 * T, T), 0) == picks[j : j + 1, :]) & (iota((2 * T, T), 1) < n)
        hot = jnp.where(hot, 1.0, 0.0).astype(BF)
        mine = core == j
        gg = jnp.where(mine, misc[3:4, :T], misc_o[3:4, :T]).astype(F32)
        gg = jnp.sum(jnp.where(eye, gg, 0.0), axis=1, keepdims=True)
        gg = nn(hot, jnp.broadcast_to(gg, (T, T)).astype(BF))[:, :1]
        forth = nn(hot, jnp.where(mine, delta[...], delta_o[...]))
        down = nn(hot, jnp.where(mine, back[...], back_o[...]))
        mixed[span, :] = (tokens[span, :].astype(F32) + forth).astype(BF)
        grad[span, :] = (cot[span, :].astype(F32) + (down + gg * wr)).astype(BF)
        for i, (v, h) in enumerate(((mixed, h_mixed), (grad, h_grad))):
            stores.append(pltpu.make_async_copy(v.at[span], h.at[span], sem.at[2 * j + i]))
            stores[-1].start()
    for store in stores:
        store.wait()


def dense_kernel(base, eighths, *refs):
    same, cross, dense, tile = refs[:4], refs[4:8], refs[8], refs[9]
    s = lax.axis_index("seq")
    core = lax.axis_index("mlp") % 2
    pos = s % 4
    first = (s // 4) * GROUP
    size = [eighths[first + i] for i in range(GROUP)]
    start = []
    for i in range(GROUP):
        total = jnp.int32(0)
        for j in range(GROUP):
            ahead = (size[j] >= size[i]) if j < i else (size[j] > size[i])
            if j != i:
                total = total + jnp.where(ahead, size[j], 0)
        start.append(total)

    def of(values, at):
        out = values[0]
        for i in range(1, GROUP):
            out = jnp.where(at == i, values[i], out)
        return out

    def put(src, seq):
        count, to = of(size, seq), of(start, seq)
        for b in range(4):

            @pl.when(b < count)
            def _():
                dst = pl.multiple_of((to + b) * BLOCK, BLOCK)
                dense[pl.ds(dst, BLOCK), :] = src[base + b * BLOCK : base + (b + 1) * BLOCK, :]

    for i in range(4):
        put(same[i], 2 * (pos ^ i) + core)
        put(cross[i], 2 * (pos ^ i) + 1 - core)
    tile[:T, :] = dense[pl.ds(pl.multiple_of((2 * (pos % 2) + core) * T, T), T), :]


def relay_kernel(*refs):
    n = len(refs) // 2
    for src, out in zip(refs[:n], refs[n:]):
        size = min(src.shape[0], out.shape[0]) // T * T
        out[:size, :] = src[:size, :]


def join_kernel(z, y, zc, yc, dense):
    pos = lax.axis_index("seq") % 2
    core = lax.axis_index("mlp") % 2
    for half, same, cross in ((pos, z, zc), (1 - pos, y, yc)):
        for src, at in ((same, 2 * half + core), (cross, 2 * half + 1 - core)):
            dense[pl.ds(pl.multiple_of(at * T, T), T), :] = src[:T, :]


def all_forward_kernel(x, g1, g2, wq, wk, wv, wo, n1, q, k, v, p, ctx, n2, raw):
    xf, attn = forward_rows(x, g1, wq, wk, wv, wo, n1, q, k, v, p, ctx, SPANS, raw, lambda i: None)
    mid = xf + attn
    n2[...] = (mid * inv_rms(mid) * row(g2)).astype(BF)


def thirds():
    step = D // 3
    return [slice(j * step, (j + 1) * step) for j in range(3)]


def grad_out(outs, bufs, tmp, sem, parts, olds):
    stores = []
    for i, (left, right) in enumerate(parts):
        for j, at in enumerate(thirds()):
            tmp[j][...] = tn(left[:, at], right[...])
            bufs[i][at, :] = tmp[j][...] + olds[i][at, :]
            stores.append(pltpu.make_async_copy(bufs[i].at[at], outs[i].at[at], sem.at[3 * i + j]))
            stores[-1].start()
    for store in stores:
        store.wait()


def mlp_rows(n2, dm, wup, wdown, act, dup):
    a, slope = gelu_both(nn(n2[...], wup[...]))
    act[...] = a.astype(BF)
    dup[...] = (slope * nt(dm[...], wdown[...])).astype(BF)


def first_mlp_kernel(n2, dm, wup, wdown, gup, gdown, act, dup):
    mlp_rows(n2, dm, wup, wdown, act, dup)
    for out, left, right in ((gdown, act, dm), (gup, n2, dup)):
        for at in thirds():
            out[at, :] = tn(left[:, at], right[...])


def last_mlp_kernel(n2, dm, wup, wdown, gup_a, gdown_a, gup, gdown, act, dup, b0, b1, t0, t1, t2, sem):
    mlp_rows(n2, dm, wup, wdown, act, dup)
    parts = ((act, dm), (n2, dup))
    grad_out((gdown, gup), (b0, b1), (t0, t1, t2), sem, parts, (gdown_a, gup_a))


def back_rows(dattn, q, k, v, p, wo, dq, dk, dv, dctx, work):
    dctx[...] = nt(dattn[...], wo[...]).astype(BF)
    attend_back(4, q, k, v, p, dctx, dq, dk, dv, *work)


def first_back_kernel(dattn, q, k, v, p, wo, dq, dk, dv, dctx, *work):
    back_rows(dattn, q, k, v, p, wo, dq, dk, dv, dctx, work)


def first_grad_kernel(dattn, n1, ctx, dq, dk, dv, gq, gk, gv, go):
    for out, left, right in ((go, ctx, dattn), (gv, n1, dv), (gk, n1, dk), (gq, n1, dq)):
        for at in thirds():
            out[at, :] = tn(left[:, at], right[...])


def last_back_kernel(
    dattn, q, k, v, p, wo, n1, ctx, gq_a, gk_a, gv_a, go_a,
    gq, gk, gv, go, dq, dk, dv, dctx, w0, w1, w2, b0, b1, b2, b3, t0, t1, t2, sem,
):
    back_rows(dattn, q, k, v, p, wo, dq, dk, dv, dctx, (w0, w1, w2))
    parts = ((ctx, dattn), (n1, dv), (n1, dk), (n1, dq))
    olds = (go_a, gv_a, gk_a, gq_a)
    grad_out((go, gv, gk, gq), (b0, b1, b2, b3), (t0, t1, t2), sem, parts, olds)


def fold_both_kernel(keep_n, keep_m, came_n, came_m, half_n, half_m):
    half_n[...] = (keep_n[...] + came_n[...].astype(F32)).astype(BF)
    half_m[...] = (keep_m[...] + came_m[...].astype(F32)).astype(BF)


def fold_kernel(a, b, out):
    out[...] = a[...] + b[...]


def halves(total):
    high = total.astype(BF).astype(F32)
    return high, (total - high).astype(BF).astype(F32)


def keep(total, rows, out):
    high, low = halves(total)
    rows[...] = jnp.concatenate([high, low], axis=0).astype(BF)
    out[...] = high + low


def read(rows):
    both = rows[...].astype(F32)
    return both[:8] + both[8:]


def unpack_kernel(mine, other, tile, out_tile, out):
    def whole(ref):
        return ref[:8, :].astype(F32) + ref[16:24, :].astype(F32)

    out_tile[:T, :] = tile[:T, :]
    keep(whole(mine) + whole(other), out_tile.at[T : T + 16], out)


def relay_fold_kernel(tile, small, out_tile, out):
    out_tile[:T, :] = tile[:T, :]
    keep(small[...] + read(tile.at[T : T + 16]), out_tile.at[T : T + 16], out)


def last_fold_kernel(a, b, o0, o1, o2):
    v = a[...] + b[...]
    for i, out in enumerate((o0, o1, o2)):
        out[...] = v[i]


LIMIT = {
    "pick_kernel": 8, "own_kernel": 24, "middle_kernel": 8, "own_back_kernel": 16,
    "place_kernel": 10, "dense_kernel": 8, "join_kernel": 6, "all_forward_kernel": 14,
    "first_mlp_kernel": 12, "last_mlp_kernel": 16, "first_back_kernel": 10, "last_back_kernel": 22,
    "first_grad_kernel": 8,
    "fold_both_kernel": 4, "fold_kernel": 4, "unpack_kernel": 4, "relay_fold_kernel": 4, "last_fold_kernel": 4,
    "relay_kernel": 4,
}


VM = pl.BlockSpec(memory_space=pltpu.VMEM)
SM = pl.BlockSpec(memory_space=pltpu.SMEM)
HB = pl.BlockSpec(memory_space=pltpu.HBM)
AN = pl.BlockSpec(memory_space=pl.ANY)


def call(
    kernel, ins, outs, scratch=(), scalars=0, after=(), through=(), hbm_in=0, hbm_out=False,
    sems=0,
):
    n, skip, m, t = len(ins), len(after), len(outs), len(through)
    name = getattr(kernel, "func", kernel).__name__

    def body(*refs):
        given, made = refs[n + skip : n + skip + t], refs[n + skip + t + m :][:t]
        for old, new in zip(given, made):
            new[...] = old[...]
        kernel(*refs[:n], *refs[n + skip + t :][:m], *refs[n + skip + t + m + t :])

    own = n - scalars - hbm_in
    return pl.pallas_call(
        body,
        name=name,
        out_shape=[jax.ShapeDtypeStruct(s, d) for s, d in outs]
        + [jax.ShapeDtypeStruct(v.shape, v.dtype) for v in through],
        in_specs=[SM] * scalars + [VM] * own + [HB] * hbm_in + [AN] * skip + [VM] * t,
        out_specs=[HB if hbm_out else VM] * m + [VM] * t,
        scratch_shapes=[like(v) for v in scratch]
        + ([pltpu.SemaphoreType.DMA((sems,))] if sems else []),
        compiler_params=pltpu.CompilerParams(vmem_limit_bytes=LIMIT[name] * MIB),
        cost_estimate=pl.CostEstimate(flops=1000, bytes_accessed=1000, transcendentals=0),
    )(*ins, *after, *through)


def like(v):
    if isinstance(v, tuple):
        return pltpu.VMEM(*v)
    return (pltpu.SMEM if v.dtype == jnp.int32 and v.ndim == 1 else pltpu.VMEM)(v.shape, v.dtype)


def far_off(v):
    return pltpu.with_memory_space_constraint(v, pltpu.HBM)


def swap(value, axis, mask):
    pairs = [(i, i ^ mask) for i in range(lax.axis_size(axis))]
    return lax.ppermute(value, axis, pairs)


def rows(n, t=BF):
    return ((n, D), t)


def probs(n):
    return ((n, PAIRS, T, 2 * T), BF)


def local(
    tokens, cotangent, picks, eighths, w_router, gain_attn, gain_mlp,
    wq, wk, wv, wo, wup, wdown,
):
    wr, g1, g2 = w_router, gain_attn, gain_mlp

    def relay(parts, after=(), through=()):
        sizes = [rows(v.shape[0] // T * T) for v in parts]
        return call(relay_kernel, parts, sizes, after=after)

    def dense(same, cross, base=0, after=(), through=(), pad=0):
        return call(
            functools.partial(dense_kernel, base), (eighths, *same, *cross),
            [rows(4 * T), rows(T + 8 * pad)], scalars=1, after=after, through=through,
        )

    def join(parts, after=()):
        return call(join_kernel, parts, [rows(4 * T)], after=after)[0]

    def core(v):
        return swap(v, "mlp", 1)

    def all_forward(x, after=(), through=()):
        return call(
            all_forward_kernel, (x, g1, g2, wq, wk, wv, wo),
            [rows(4 * T)] * 4 + [probs(4)] + [rows(4 * T)] * 2, FORE, after=after, through=through,
        )

    def fold(v, mask, after=()):
        return call(fold_kernel, (v, swap(v, "seq", mask)), [rows(8, F32)], after=after)[0]

    xr, cr, dm, mine, other, tokens, cotangent = call(
        pick_kernel, [far_off(v) for v in (eighths, picks, tokens, cotangent, wr)],
        [rows(2 * T)] * 3 + [rows(2 * T + XD), rows(2 * T)] + [rows(4 * T)] * 2,
        [eighths, picks, wr], hbm_in=5, sems=5,
    )
    near = [swap(mine, "seq", k) for k in (1, 2, 3)]
    keep_n, keep_m, send_n, send_m, qc, kc, vc, pc, ac = call(
        own_kernel, (xr, dm, *(far_off(v) for v in (g1, g2, wq, wk, wv, wo, wup, wdown))),
        [rows(T, F32)] * 2 + [rows(T)] * 5 + [probs(1), rows(T, F32)],
        [rows(2 * T)] * 4 + [probs(2), rows(2 * T), rows(2 * T, F32)] + [rows(2 * T)] * 3
        + FORE + [g1, g2] + [rows(D)] * 6, hbm_in=8, sems=8,
    )
    half_n, half_m = call(
        fold_both_kernel, (keep_n, keep_m, core(send_n), core(send_m)), [rows(T)] * 2
    )
    both_n = swap(half_n, "mlp", 2)
    dattn, dmid, small, half_m = call(
        middle_kernel, (half_n, both_n, xr, cr, ac, g2, wr),
        [rows(T + 16), rows(T, F32), ((1, D), F32)], through=(half_m,),
    )
    a1, a2, a3 = [swap(dattn, "seq", k) for k in (1, 2, 3)]
    both_m = swap(half_m, "mlp", 2)
    near = relay(near, after=(dattn,))
    same, cross = (mine, *near), (other, *(core(v) for v in near))
    x_a, x_tile = dense(same, cross, pad=2)
    far_x = swap(x_tile, "seq", 4)
    n1_a, q_a, k_a, v_a, p_a, ctx_a, n2_a = all_forward(x_a)
    res = call(
        own_back_kernel,
        (dattn, dmid, small, half_m, both_m, xr, cr, ac, qc, kc, vc, pc, g1, wr, wq, wk, wv, wo),
        [rows(T), rows(T), rows(32)], [rows(T)] * 4 + BACK, after=(n2_a,),
    )
    same_a = relay([dattn, a1, a2, a3], after=(res[0],))
    cross_a = [core(v) for v in same_a]
    d_a, d_tile = dense(same, cross, base=T, after=(same_a[0],))
    a_a, a_tile = dense(same_a, cross_a, after=(d_a,), pad=1)
    far_a = swap(a_tile, "seq", 4)
    (far_x,) = relay([far_x], after=(a_a,))
    near_x, cross_x = swap(far_x, "seq", 1), core(far_x)
    dq_a, dk_a, dv_a, *res = call(
        first_back_kernel, (a_a, q_a, k_a, v_a, p_a, wo), [rows(4 * T)] * 3,
        [rows(4 * T)] + BACK, after=(far_x,), through=res,
    )
    other = [core(v) for v in res]
    ups = call(
        first_mlp_kernel, (n2_a, d_a, wup, wdown), [rows(D, F32)] * 2, [rows(4 * T)] * 2,
        after=(dq_a,),
    )
    *grads, d_tile = call(
        first_grad_kernel, (a_a, n1_a, ctx_a, dq_a, dk_a, dv_a), [rows(D, F32)] * 4,
        after=(ups[0],), through=(d_tile,),
    )
    d_tile, small = call(
        unpack_kernel, (res[2], other[2], d_tile), [rows(T + 16), rows(8, F32)]
    )
    far_d = swap(d_tile, "seq", 4)
    (far_a,) = relay([far_a], after=(small,))
    near_a, cross_a = swap(far_a, "seq", 1), core(far_a)
    near_x, cross_x = relay([near_x, cross_x], after=(far_a,))
    next_x = core(near_x)
    n1_b, q_b, k_b, v_b, p_b, ctx_b, n2_b = all_forward(
        join((far_x, near_x, cross_x, next_x))
    )
    near_a, cross_a = relay([near_a, cross_a], after=(n2_b,))
    next_a = core(near_a)
    mixed, grad_tokens, small = call(
        place_kernel, (eighths, picks, wr, *res, *other, tokens, cotangent),
        [rows(4 * T)] * 2, [rows(4 * T)] * 2, scalars=1, hbm_out=True, sems=4,
        through=(small,), after=(near_a,),
    )
    far_d, small = call(relay_fold_kernel, (far_d, small), [rows(T + 16), rows(8, F32)])
    near_d, cross_d = swap(far_d, "seq", 1), core(far_d)
    a_b = join((far_a, near_a, cross_a, next_a), after=(far_d,))
    gq, gk, gv, go, token = call(
        last_back_kernel, (a_b, q_b, k_b, v_b, p_b, wo, n1_b, ctx_b, *grads),
        [rows(D, F32)] * 4,
        [rows(4 * T)] * 4 + BACK + [rows(D, F32)] * 4 + [rows(D // 3, F32)] * 3,
        hbm_out=True, sems=12, through=(small,),
    )
    near_d, small = call(
        relay_fold_kernel, (near_d, small), [rows(T + 16), rows(8, F32)], after=(token,)
    )
    d_b = join((far_d, near_d, cross_d, core(near_d)))
    gup, gdown, token = call(
        last_mlp_kernel, (n2_b, d_b, wup, wdown, *ups), [rows(D, F32)] * 2,
        [rows(4 * T)] * 2 + [rows(D, F32)] * 2 + [rows(D // 3, F32)] * 3,
        hbm_out=True, sems=6, through=(small,),
    )
    mask = lax.axis_size("seq") // 2
    while mask > 4:
        small = fold(small, mask)
        mask //= 2
    smalls = call(
        last_fold_kernel, (small, swap(small, "seq", 2)), [((D,), F32)] * 3, after=(token,)
    )
    total = [gq, gk, gv, go, gup, gdown]
    mask = 8
    while mask < lax.axis_size("seq"):
        total = [g + swap(g, "seq", mask) for g in total]
        mask *= 2
    return (mixed, grad_tokens, *smalls, *total)


def solution(mesh):
    rows, cols, split, full = P("seq", None), P(None, "mlp"), P("mlp", None), P()
    return jax.shard_map(
        local,
        mesh=mesh,
        in_specs=(rows, rows, rows) + (full,) * 8 + (cols, split),
        out_specs=(rows, rows) + (full,) * 7 + (cols, split),
        check_vma=False,
    )
```

```python
import functools

import jax
import jax.numpy as jnp
from jax import lax
from jax.experimental import pallas as pl
from jax.experimental.pallas import tpu as pltpu
from jax.sharding import PartitionSpec as P

F32 = jnp.float32
BF = jnp.bfloat16
EPS = 1e-06
NEG = -1e30
SCALE = 0.125
D = 768
T = 128
PAIRS = 6
GROUP = 8
BLOCK = 32
MIB = 2**20
XD = 16


def nn(a, b):
    return lax.dot_general(a, b, (((1,), (0,)), ((), ())), preferred_element_type=F32)


def nt(a, b):
    return lax.dot_general(a, b, (((1,), (1,)), ((), ())), preferred_element_type=F32)


def tn(a, b):
    return lax.dot_general(a, b, (((0,), (0,)), ((), ())), preferred_element_type=F32)


def iota(shape, dim):
    return lax.broadcasted_iota(jnp.int32, shape, dim)


def row(ref):
    return ref[...].astype(F32).reshape(1, D)


def inv_rms(v):
    return lax.rsqrt(jnp.mean(v * v, axis=-1, keepdims=True) + EPS)


def causal(span):
    keys, queries = iota((T, 2 * T), 0), iota((T, 2 * T), 1) % T
    return (keys <= queries) & (keys // span == queries // span)


def first_head():
    return iota((T, T), 1) < 64


def two_heads(v):
    zero = jnp.zeros((), BF)
    low = first_head()
    return jnp.concatenate([jnp.where(low, v, zero), jnp.where(low, zero, v)], axis=0)


def one_pair(v):
    return jnp.where(first_head(), v[:T], v[T:])


def stagger(count, stages):
    for n in range(count + len(stages) - 1):
        for s, stage in enumerate(stages):
            if 0 <= n - s < count:
                stage(n - s, (n - s) % 4)


def place_of(n):
    return n // PAIRS, n % PAIRS, (tile_at(n // PAIRS), tile_at(n % PAIRS))


def attend(q, k, v, p, ctx, spans, raw):
    def score(n, slot):
        i, j, at = place_of(n)
        raw[slot] = nt(k[at], two_heads(q[at]))

    def softmax(n, slot):
        i, j, at = place_of(n)
        s = jnp.where(causal(spans[i]), raw[slot] * SCALE, NEG)
        e = jnp.exp(s - jnp.max(s, axis=0, keepdims=True))
        p[i, j] = (e * (1.0 / jnp.sum(e, axis=0, keepdims=True))).astype(BF)

    def mix(n, slot):
        i, j, at = place_of(n)
        ctx[at] = one_pair(tn(p[i, j], v[at])).astype(BF)

    stagger(len(spans) * PAIRS, (score, softmax, mix))


def attend_back(tiles, q, k, v, p, dctx, dq, dk, dv, wide, raw, ds):
    def score(n, slot):
        i, j, at = place_of(n)
        wide[slot] = two_heads(dctx[at])
        raw[slot] = nt(v[at], wide[slot])

    def softmax(n, slot):
        i, j, at = place_of(n)
        pf, dp = p[i, j].astype(F32), raw[slot]
        ds[slot] = (pf * (dp - jnp.sum(pf * dp, axis=0, keepdims=True))).astype(BF)
        dv[at] = nn(p[i, j], wide[slot]).astype(BF)

    def mix(n, slot):
        i, j, at = place_of(n)
        dk[at] = (nn(ds[slot], two_heads(q[at])) * SCALE).astype(BF)
        dq[at] = (one_pair(tn(ds[slot], k[at])) * SCALE).astype(BF)

    stagger(tiles * PAIRS, (score, softmax, mix))


FORE = [((4, T, 2 * T), F32)]
BACK = [((4, 2 * T, T), BF), ((4, T, 2 * T), F32), ((4, T, 2 * T), BF)]


def gelu_both(u):
    c = 0.7978845608028654
    u2 = u * u
    t = jnp.tanh(c * u * (1.0 + 0.044715 * u2))
    half = 0.5 * (1.0 + t)
    slope = half + 0.5 * u * (1.0 - t * t) * (c * (1.0 + 3.0 * 0.044715 * u2))
    return u * half, slope


def tile_at(i):
    return slice(i * T, (i + 1) * T)


SPANS = (128, 128, 64, 32)


def forward_rows(x_ref, g1, wq, wk, wv, wo, n1, q, k, v, p, ctx, spans, raw, ready):
    xf = x_ref[...].astype(F32)
    n1[...] = (xf * inv_rms(xf) * row(g1)).astype(BF)
    for i, (out, w) in enumerate(((q, wq), (k, wk), (v, wv))):
        ready(i)
        out[...] = nn(n1[...], w[...]).astype(BF)
    attend(q, k, v, p, ctx, spans, raw)
    ready(3)
    return xf, nn(ctx[...], wo[...])


def pick_kernel(
    h_eighths, h_picks, h_tokens, h_cot, h_router, h_wq,
    xr, cr, dm, mine, other, tokens, cot, wq,
    eighths, picks, w_router, sem,
):
    pairs = (
        (h_eighths, eighths), (h_picks, picks), (h_tokens, tokens),
        (h_router, w_router), (h_cot, cot), (h_wq, wq),
    )
    loads = [pltpu.make_async_copy(h, v, sem.at[i]) for i, (h, v) in enumerate(pairs)]
    for load in loads:
        load.start()
    for load in loads[:5]:
        load.wait()
    s = lax.axis_index("seq")
    core = lax.axis_index("mlp") % 2
    eye = iota((T, T), 0) == iota((T, T), 1)
    for j in range(2):
        n = eighths[2 * s + j] * BLOCK
        col = jnp.sum(jnp.where(eye, picks[j : j + 1, :], 0), axis=1, keepdims=True)
        hot = (iota((T, 2 * T), 1) == col) & (iota((T, 2 * T), 0) < n)
        hot = jnp.where(hot, 1.0, 0.0).astype(BF)
        span = slice(2 * T * j, 2 * T * (j + 1))
        x = nn(hot, tokens[span, :])
        c = nn(hot, cot[span, :])
        gate = jnp.sum(x * row(w_router), axis=-1, keepdims=True)
        d = (gate.astype(BF).astype(F32) * c).astype(BF)
        xr[tile_at(j), :] = x.astype(BF)
        cr[tile_at(j), :] = c.astype(BF)
        dm[tile_at(j), :] = d

        for out, own in ((mine, core == j), (other, core != j)):

            @pl.when(own)
            def _():
                out[:T, :] = x.astype(BF)
                out[T : 2 * T, :] = d
    loads[5].wait()


def own_kernel(
    xr, dm, wq, hg1, hg2, hk, hv, ho, hup, hdown,
    keep, send, q, k, v, p, att, act, wk, wv, wo, wup, wdown,
    n1, ctx, n2, dup, raw, g1, g2, sem,
):
    core = lax.axis_index("mlp") % 2
    pairs = ((hg1, g1), (hk, wk), (hv, wv), (ho, wo), (hup, wup), (hdown, wdown), (hg2, g2))
    loads = [pltpu.make_async_copy(h, w, sem.at[i]) for i, (h, w) in enumerate(pairs)]
    for i in (0, 1, 2, 6):
        loads[i].start()
    loads[0].wait()

    def ready(i):
        if i == 0:
            for j in (3, 4, 5):
                loads[j].start()
        else:
            loads[i].wait()

    xf, attn = forward_rows(xr, g1, wq, wk, wv, wo, n1, q, k, v, p, ctx, (T, T), raw, ready)
    loads[6].wait()
    att[...] = attn
    mid = xf + attn
    n2[...] = (mid * inv_rms(mid) * row(g2)).astype(BF)
    loads[4].wait()
    a, slope = gelu_both(nn(n2[...], wup[...]))
    act[...] = a.astype(BF)
    loads[5].wait()
    dup[...] = (slope * nt(dm[...], wdown[...])).astype(BF)
    share(core, nt(dup[...], wup[...]), keep, send)


def share(core, both, keep, send):
    for j in range(2):

        @pl.when(core == j)
        def _():
            keep[...] = both[tile_at(j), :]
            send[...] = both[tile_at(1 - j), :].astype(BF)


def own_out_kernel(act, wdown, keep, send):
    share(lax.axis_index("mlp") % 2, nn(act[...], wdown[...]), keep, send)


def middle_kernel(dna, dnb, xr, cr, ac, g2, w_router, dattn, dmid_out, small):
    core = lax.axis_index("mlp") % 2
    rows = pl.ds(core * T, T)
    x = xr[rows, :].astype(F32)
    gate = jnp.sum(x * row(w_router), axis=-1, keepdims=True)
    gate = gate.astype(BF).astype(F32)
    mid = x + ac[rows, :]
    r = inv_rms(mid)
    unit = mid * r
    dn = dna[...].astype(F32) + dnb[...].astype(F32)
    small[...] = jnp.sum(dn * unit, axis=0, keepdims=True)
    scaled = dn * row(g2)
    dmid = r * (scaled - unit * jnp.mean(scaled * unit, axis=-1, keepdims=True))
    dmid_out[...] = dmid
    dattn[:T, :] = (gate * cr[rows, :].astype(F32) + dmid).astype(BF)


def own_back_kernel(
    dattn, dmid, small_in, moa, mob, xr, cr, ac, qc, kc, vc, pc, g1, w_router, wq, wk, wv, wo,
    delta, back, misc, dctx, dq, dk, dv, *work,
):
    core = lax.axis_index("mlp") % 2
    rows = pl.ds(core * T, T)
    x = xr[rows, :].astype(F32)
    wr = row(w_router)
    gate = jnp.sum(x * wr, axis=-1, keepdims=True).astype(BF).astype(F32)
    branch = ac[rows, :] + (moa[...].astype(F32) + mob[...].astype(F32))
    gg = jnp.sum(cr[rows, :].astype(F32) * branch, axis=-1, keepdims=True).astype(BF)
    delta[...] = (gate * branch).astype(BF)
    dctx[...] = nt(dattn[:T, :], wo[...]).astype(BF)
    q, k, v = (ref.at[rows, :] for ref in (qc, kc, vc))
    attend_back(1, q, k, v, pc.at[pl.ds(core, 1)], dctx, dq, dk, dv, *work)
    dn = nt(dq[...], wq[...]) + nt(dk[...], wk[...]) + nt(dv[...], wv[...])
    r = inv_rms(x)
    unit = x * r
    scaled = dn * row(g1)
    dx = r * (scaled - unit * jnp.mean(scaled * unit, axis=-1, keepdims=True))
    back[...] = (dmid[...] + dx).astype(BF)
    eye = iota((T, T), 0) == iota((T, T), 1)
    across = jnp.sum(jnp.where(eye, gg.astype(F32), 0.0), axis=0, keepdims=True)
    total = jnp.concatenate(
        [
            jnp.sum(gg.astype(F32) * x, axis=0, keepdims=True),
            jnp.sum(dn * unit, axis=0, keepdims=True),
            small_in[...],
            jnp.concatenate([across, jnp.zeros((1, D - T), F32)], axis=1),
            jnp.zeros((12, D), F32),
        ],
        axis=0,
    )
    high = total.astype(BF)
    misc[:16, :] = high
    misc[16:, :] = (total - high.astype(F32)).astype(BF)


def place_kernel(
    eighths, picks, w_router, delta, back, misc, delta_o, back_o, misc_o, tokens, cot,
    h_mixed, h_grad, mixed, grad, sem,
):
    s = lax.axis_index("seq")
    core = lax.axis_index("mlp") % 2
    wr = row(w_router)
    spans = [slice(2 * T * j, 2 * T * (j + 1)) for j in range(2)]
    stores = []
    eye = iota((T, T), 0) == iota((T, T), 1)
    for j, span in enumerate(spans):
        n = eighths[2 * s + j] * BLOCK
        hot = (iota((2 * T, T), 0) == picks[j : j + 1, :]) & (iota((2 * T, T), 1) < n)
        hot = jnp.where(hot, 1.0, 0.0).astype(BF)
        mine = core == j
        gg = jnp.where(mine, misc[3:4, :T], misc_o[3:4, :T]).astype(F32)
        gg = jnp.sum(jnp.where(eye, gg, 0.0), axis=1, keepdims=True)
        gg = nn(hot, jnp.broadcast_to(gg, (T, T)).astype(BF))[:, :1]
        forth = nn(hot, jnp.where(mine, delta[...], delta_o[...]))
        down = nn(hot, jnp.where(mine, back[...], back_o[...]))
        mixed[span, :] = (tokens[span, :].astype(F32) + forth).astype(BF)
        grad[span, :] = (cot[span, :].astype(F32) + (down + gg * wr)).astype(BF)
        for i, (v, h) in enumerate(((mixed, h_mixed), (grad, h_grad))):
            stores.append(pltpu.make_async_copy(v.at[span], h.at[span], sem.at[2 * j + i]))
            stores[-1].start()
    for store in stores:
        store.wait()


def dense_kernel(base, eighths, *refs):
    same, cross, dense, tile = refs[:4], refs[4:8], refs[8], refs[9]
    s = lax.axis_index("seq")
    core = lax.axis_index("mlp") % 2
    pos = s % 4
    first = (s // 4) * GROUP
    size = [eighths[first + i] for i in range(GROUP)]
    start = []
    for i in range(GROUP):
        total = jnp.int32(0)
        for j in range(GROUP):
            ahead = (size[j] >= size[i]) if j < i else (size[j] > size[i])
            if j != i:
                total = total + jnp.where(ahead, size[j], 0)
        start.append(total)

    def of(values, at):
        out = values[0]
        for i in range(1, GROUP):
            out = jnp.where(at == i, values[i], out)
        return out

    def put(src, seq):
        count, to = of(size, seq), of(start, seq)

        def move(first, last):
            dst = pl.multiple_of((to + first) * BLOCK, BLOCK)
            span = (last - first) * BLOCK
            dense[pl.ds(dst, span), :] = src[base + first * BLOCK : base + last * BLOCK, :]

        move(0, 1)
        pl.when(count >= 2)(lambda: move(1, 2))
        pl.when(count >= 4)(lambda: move(2, 4))

    for i in range(4):
        put(same[i], 2 * (pos ^ i) + core)
        put(cross[i], 2 * (pos ^ i) + 1 - core)
    tile[:T, :] = dense[pl.ds(pl.multiple_of((2 * (pos % 2) + core) * T, T), T), :]


def relay_kernel(*refs):
    n = len(refs) // 2
    for src, out in zip(refs[:n], refs[n:]):
        size = min(src.shape[0], out.shape[0]) // T * T
        out[:size, :] = src[:size, :]


def join_kernel(z, y, zc, yc, dense):
    pos = lax.axis_index("seq") % 2
    core = lax.axis_index("mlp") % 2
    for half, same, cross in ((pos, z, zc), (1 - pos, y, yc)):
        for src, at in ((same, 2 * half + core), (cross, 2 * half + 1 - core)):
            dense[pl.ds(pl.multiple_of(at * T, T), T), :] = src[:T, :]


def all_forward_kernel(x, g1, g2, wq, wk, wv, wo, n1, q, k, v, p, ctx, n2, raw):
    xf, attn = forward_rows(x, g1, wq, wk, wv, wo, n1, q, k, v, p, ctx, SPANS, raw, lambda i: None)
    mid = xf + attn
    n2[...] = (mid * inv_rms(mid) * row(g2)).astype(BF)


def thirds():
    step = D // 3
    return [slice(j * step, (j + 1) * step) for j in range(3)]


def grad_out(outs, bufs, tmp, sem, parts, olds, first):
    stores = []
    for i, (left, right) in enumerate(parts):
        for j, at in enumerate(thirds()):
            tmp[j][...] = tn(left[:, at], right[...])
            bufs[i][at, :] = tmp[j][...] + olds[i][at, :]
            stores.append(pltpu.make_async_copy(bufs[i].at[at], outs[i].at[at], sem.at[first + 3 * i + j]))
            stores[-1].start()
    return stores


def mlp_rows(n2, dm, wup, wdown, act, dup):
    a, slope = gelu_both(nn(n2[...], wup[...]))
    act[...] = a.astype(BF)
    dup[...] = (slope * nt(dm[...], wdown[...])).astype(BF)


def first_mlp_kernel(n2, dm, wup, wdown, gup, gdown, act, dup):
    mlp_rows(n2, dm, wup, wdown, act, dup)
    for out, left, right in ((gdown, act, dm), (gup, n2, dup)):
        for at in thirds():
            out[at, :] = tn(left[:, at], right[...])


def last_mlp_kernel(n2, dm, wup, wdown, gup_a, gdown_a, gup, gdown, act, dup, b0, b1, t0, t1, t2, sem):
    mlp_rows(n2, dm, wup, wdown, act, dup)
    parts = ((act, dm), (n2, dup))
    for store in grad_out((gdown, gup), (b0, b1), (t0, t1, t2), sem, parts, (gdown_a, gup_a), 0):
        store.wait()


def back_rows(dattn, q, k, v, p, wo, dq, dk, dv, dctx, work):
    dctx[...] = nt(dattn[...], wo[...]).astype(BF)
    attend_back(4, q, k, v, p, dctx, dq, dk, dv, *work)


def first_back_kernel(dattn, q, k, v, p, wo, dq, dk, dv, dctx, *work):
    back_rows(dattn, q, k, v, p, wo, dq, dk, dv, dctx, work)


def first_grad_kernel(dattn, n1, ctx, dq, dk, dv, gq, gk, gv, go):
    for out, left, right in ((go, ctx, dattn), (gv, n1, dv), (gk, n1, dk), (gq, n1, dq)):
        for at in thirds():
            out[at, :] = tn(left[:, at], right[...])


def last_back_kernel(
    dattn, q, k, v, p, wo, n1, ctx, gq_a, gk_a, gv_a, go_a,
    gq, gk, gv, go, dq, dk, dv, dctx, w0, w1, w2, b0, b1, b2, b3, t0, t1, t2, sem,
):
    stores = grad_out((go,), (b0,), (t0, t1, t2), sem, ((ctx, dattn),), (go_a,), 0)
    back_rows(dattn, q, k, v, p, wo, dq, dk, dv, dctx, (w0, w1, w2))
    parts, olds = ((n1, dv), (n1, dk), (n1, dq)), (gv_a, gk_a, gq_a)
    stores += grad_out((gv, gk, gq), (b1, b2, b3), (t0, t1, t2), sem, parts, olds, 3)
    for store in stores:
        store.wait()


def fold_half_kernel(keep, came, half):
    half[...] = (keep[...] + came[...].astype(F32)).astype(BF)


def fold_kernel(a, b, out):
    out[...] = a[...] + b[...]


def halves(total):
    high = total.astype(BF).astype(F32)
    return high, (total - high).astype(BF).astype(F32)


def keep(total, rows, out):
    high, low = halves(total)
    rows[...] = jnp.concatenate([high, low], axis=0).astype(BF)
    out[...] = high + low


def read(rows):
    both = rows[...].astype(F32)
    return both[:8] + both[8:]


def unpack_kernel(mine, other, tile, out_tile, out):
    def whole(ref):
        return ref[:8, :].astype(F32) + ref[16:24, :].astype(F32)

    out_tile[:T, :] = tile[:T, :]
    keep(whole(mine) + whole(other), out_tile.at[T : T + 16], out)


def relay_fold_kernel(tile, small, out_tile, out):
    out_tile[:T, :] = tile[:T, :]
    keep(small[...] + read(tile.at[T : T + 16]), out_tile.at[T : T + 16], out)


def last_fold_kernel(a, b, o0, o1, o2):
    v = a[...] + b[...]
    for i, out in enumerate((o0, o1, o2)):
        out[...] = v[i]


LIMIT = {
    "pick_kernel": 8, "own_kernel": 24, "middle_kernel": 8, "own_back_kernel": 16,
    "place_kernel": 10, "dense_kernel": 8, "join_kernel": 6, "all_forward_kernel": 14,
    "first_mlp_kernel": 12, "last_mlp_kernel": 16, "first_back_kernel": 10, "last_back_kernel": 22,
    "first_grad_kernel": 8,
    "fold_half_kernel": 4, "own_out_kernel": 6, "fold_kernel": 4, "unpack_kernel": 4, "relay_fold_kernel": 4, "last_fold_kernel": 4,
    "relay_kernel": 4,
}


VM = pl.BlockSpec(memory_space=pltpu.VMEM)
SM = pl.BlockSpec(memory_space=pltpu.SMEM)
HB = pl.BlockSpec(memory_space=pltpu.HBM)
AN = pl.BlockSpec(memory_space=pl.ANY)


def call(
    kernel, ins, outs, scratch=(), scalars=0, after=(), through=(), hbm_in=0, hbm_out=False,
    sems=0,
):
    n, skip, m, t = len(ins), len(after), len(outs), len(through)
    name = getattr(kernel, "func", kernel).__name__

    def body(*refs):
        given, made = refs[n + skip : n + skip + t], refs[n + skip + t + m :][:t]
        for old, new in zip(given, made):
            new[...] = old[...]
        kernel(*refs[:n], *refs[n + skip + t :][:m], *refs[n + skip + t + m + t :])

    own = n - scalars - hbm_in
    return pl.pallas_call(
        body,
        name=name,
        out_shape=[jax.ShapeDtypeStruct(s, d) for s, d in outs]
        + [jax.ShapeDtypeStruct(v.shape, v.dtype) for v in through],
        in_specs=[SM] * scalars + [VM] * own + [HB] * hbm_in + [AN] * skip + [VM] * t,
        out_specs=[HB if hbm_out else VM] * m + [VM] * t,
        scratch_shapes=[like(v) for v in scratch]
        + ([pltpu.SemaphoreType.DMA((sems,))] if sems else []),
        compiler_params=pltpu.CompilerParams(vmem_limit_bytes=LIMIT[name] * MIB),
        cost_estimate=pl.CostEstimate(flops=1000, bytes_accessed=1000, transcendentals=0),
    )(*ins, *after, *through)


def like(v):
    if isinstance(v, tuple):
        return pltpu.VMEM(*v)
    return (pltpu.SMEM if v.dtype == jnp.int32 and v.ndim == 1 else pltpu.VMEM)(v.shape, v.dtype)


def far_off(v):
    return pltpu.with_memory_space_constraint(v, pltpu.HBM)


def swap(value, axis, mask):
    pairs = [(i, i ^ mask) for i in range(lax.axis_size(axis))]
    return lax.ppermute(value, axis, pairs)


def rows(n, t=BF):
    return ((n, D), t)


def probs(n):
    return ((n, PAIRS, T, 2 * T), BF)


def local(
    tokens, cotangent, picks, eighths, w_router, gain_attn, gain_mlp,
    wq, wk, wv, wo, wup, wdown,
):
    wr, g1, g2 = w_router, gain_attn, gain_mlp

    def relay(parts, after=(), through=()):
        sizes = [rows(v.shape[0] // T * T) for v in parts]
        return call(relay_kernel, parts, sizes, after=after)

    def dense(same, cross, base=0, after=(), through=(), pad=0):
        return call(
            functools.partial(dense_kernel, base), (eighths, *same, *cross),
            [rows(4 * T), rows(T + 8 * pad)], scalars=1, after=after, through=through,
        )

    def join(parts, after=()):
        return call(join_kernel, parts, [rows(4 * T)], after=after)[0]

    def core(v):
        return swap(v, "mlp", 1)

    def all_forward(x, after=(), through=()):
        return call(
            all_forward_kernel, (x, g1, g2, wq, wk, wv, wo),
            [rows(4 * T)] * 4 + [probs(4)] + [rows(4 * T)] * 2, FORE, after=after, through=through,
        )

    def fold(v, mask, after=()):
        return call(fold_kernel, (v, swap(v, "seq", mask)), [rows(8, F32)], after=after)[0]

    xr, cr, dm, mine, other, tokens, cotangent, wq = call(
        pick_kernel, [far_off(v) for v in (eighths, picks, tokens, cotangent, wr, wq)],
        [rows(2 * T)] * 3 + [rows(2 * T + XD), rows(2 * T)] + [rows(4 * T)] * 2 + [rows(D)],
        [eighths, picks, wr], hbm_in=6, sems=6,
    )
    near = [swap(mine, "seq", k) for k in (1, 2, 3)]
    keep_n, send_n, qc, kc, vc, pc, ac, act, wk, wv, wo, wup, wdown = call(
        own_kernel, (xr, dm, wq, *(far_off(v) for v in (g1, g2, wk, wv, wo, wup, wdown))),
        [rows(T, F32), rows(T)] + [rows(2 * T)] * 3
        + [probs(2), rows(2 * T, F32), rows(2 * T)] + [rows(D)] * 5,
        [rows(2 * T)] * 4 + FORE + [g1, g2], hbm_in=7, sems=7,
    )
    keep_m, send_m = call(own_out_kernel, (act, wdown), [rows(T, F32), rows(T)])
    (half_n,) = call(
        fold_half_kernel, (keep_n, core(send_n)), [rows(T)], after=(keep_m,)
    )
    (half_m,) = call(
        fold_half_kernel, (keep_m, core(send_m)), [rows(T)], after=(half_n,)
    )
    both_n = swap(half_n, "mlp", 2)
    dattn, dmid, small, half_m = call(
        middle_kernel, (half_n, both_n, xr, cr, ac, g2, wr),
        [rows(T + 16), rows(T, F32), ((1, D), F32)], through=(half_m,),
    )
    a1, a2, a3 = [swap(dattn, "seq", k) for k in (1, 2, 3)]
    both_m = swap(half_m, "mlp", 2)
    near = relay(near, after=(dattn,))
    same, cross = (mine, *near), (other, *(core(v) for v in near))
    x_a, x_tile = dense(same, cross, pad=2)
    far_x = swap(x_tile, "seq", 4)
    n1_a, q_a, k_a, v_a, p_a, ctx_a, n2_a = all_forward(x_a)
    res = call(
        own_back_kernel,
        (dattn, dmid, small, half_m, both_m, xr, cr, ac, qc, kc, vc, pc, g1, wr, wq, wk, wv, wo),
        [rows(T), rows(T), rows(32)], [rows(T)] * 4 + BACK, after=(n2_a,),
    )
    same_a = relay([dattn, a1, a2, a3], after=(res[0],))
    cross_a = [core(v) for v in same_a]
    d_a, d_tile = dense(same, cross, base=T, after=(same_a[0],))
    a_a, a_tile = dense(same_a, cross_a, after=(d_a,), pad=2)
    far_a = swap(a_tile, "seq", 4)
    (far_x,) = relay([far_x], after=(a_a,))
    near_x = swap(far_x, "seq", 1)
    dq_a, dk_a, dv_a, *res = call(
        first_back_kernel, (a_a, q_a, k_a, v_a, p_a, wo), [rows(4 * T)] * 3,
        [rows(4 * T)] + BACK, after=(far_x,), through=res,
    )
    other = [core(v) for v in res]
    ups = call(
        first_mlp_kernel, (n2_a, d_a, wup, wdown), [rows(D, F32)] * 2, [rows(4 * T)] * 2,
        after=(dq_a,),
    )
    d_tile, small = call(
        unpack_kernel, (res[2], other[2], d_tile), [rows(T + 16), rows(8, F32)], after=(ups[0],)
    )
    far_d = swap(d_tile, "seq", 4)
    mixed, grad_tokens, small = call(
        place_kernel, (eighths, picks, wr, *res, *other, tokens, cotangent),
        [rows(4 * T)] * 2, [rows(4 * T)] * 2, scalars=1, hbm_out=True, sems=4,
        through=(small,),
    )
    grads = call(
        first_grad_kernel, (a_a, n1_a, ctx_a, dq_a, dk_a, dv_a), [rows(D, F32)] * 4,
        after=(small,),
    )
    (far_a,) = relay([far_a], after=(grads[0],))
    near_a = swap(far_a, "seq", 1)
    far_x, near_x = relay([far_x, near_x], after=(far_a,))
    cross_x, next_x = core(far_x), core(near_x)
    n1_b, q_b, k_b, v_b, p_b, ctx_b, n2_b = all_forward(
        join((far_x, near_x, cross_x, next_x))
    )
    far_d, small = call(
        relay_fold_kernel, (far_d, small), [rows(T + 16), rows(8, F32)], after=(n2_b,)
    )
    near_d, cross_d = swap(far_d, "seq", 1), core(far_d)
    far_a, near_a = relay([far_a, near_a], after=(small,))
    cross_a, next_a = core(far_a), core(near_a)
    a_b = join((far_a, near_a, cross_a, next_a))
    gq, gk, gv, go, token = call(
        last_back_kernel, (a_b, q_b, k_b, v_b, p_b, wo, n1_b, ctx_b, *grads),
        [rows(D, F32)] * 4,
        [rows(4 * T)] * 4 + BACK + [rows(D, F32)] * 4 + [rows(D // 3, F32)] * 3,
        hbm_out=True, sems=12, through=(small,),
    )
    near_d, small = call(
        relay_fold_kernel, (near_d, small), [rows(T + 16), rows(8, F32)], after=(token,)
    )
    d_b = join((far_d, near_d, cross_d, core(near_d)))
    gup, gdown, token = call(
        last_mlp_kernel, (n2_b, d_b, wup, wdown, *ups), [rows(D, F32)] * 2,
        [rows(4 * T)] * 2 + [rows(D, F32)] * 2 + [rows(D // 3, F32)] * 3,
        hbm_out=True, sems=6, through=(small,),
    )
    mask = lax.axis_size("seq") // 2
    while mask > 4:
        small = fold(small, mask)
        mask //= 2
    smalls = call(
        last_fold_kernel, (small, swap(small, "seq", 2)), [((D,), F32)] * 3, after=(token,)
    )
    total = [gq, gk, gv, go, gup, gdown]
    mask = 8
    while mask < lax.axis_size("seq"):
        total = [g + swap(g, "seq", mask) for g in total]
        mask *= 2
    return (mixed, grad_tokens, *smalls, *total)


def solution(mesh):
    rows, cols, split, full = P("seq", None), P(None, "mlp"), P("mlp", None), P()
    return jax.shard_map(
        local,
        mesh=mesh,
        in_specs=(rows, rows, rows) + (full,) * 8 + (cols, split),
        out_specs=(rows, rows) + (full,) * 7 + (cols, split),
        check_vma=False,
    )
```

```python
import functools

import jax
import jax.numpy as jnp
from jax import lax
from jax.experimental import pallas as pl
from jax.experimental.pallas import tpu as pltpu
from jax.sharding import PartitionSpec as P

F32 = jnp.float32
BF = jnp.bfloat16
EPS = 1e-06
NEG = -1e30
SCALE = 0.125
D = 768
T = 128
PAIRS = 6
GROUP = 8
BLOCK = 32
MIB = 2**20
XD = 8


def nn(a, b):
    return lax.dot_general(a, b, (((1,), (0,)), ((), ())), preferred_element_type=F32)


def nt(a, b):
    return lax.dot_general(a, b, (((1,), (1,)), ((), ())), preferred_element_type=F32)


def tn(a, b):
    return lax.dot_general(a, b, (((0,), (0,)), ((), ())), preferred_element_type=F32)


def iota(shape, dim):
    return lax.broadcasted_iota(jnp.int32, shape, dim)


def row(ref):
    return ref[...].astype(F32).reshape(1, D)


def inv_rms(v):
    return lax.rsqrt(jnp.mean(v * v, axis=-1, keepdims=True) + EPS)


def causal(span):
    keys, queries = iota((T, 2 * T), 0), iota((T, 2 * T), 1) % T
    return (keys <= queries) & (keys // span == queries // span)


def first_head():
    return iota((T, T), 1) < 64


def two_heads(v):
    zero = jnp.zeros((), BF)
    low = first_head()
    return jnp.concatenate([jnp.where(low, v, zero), jnp.where(low, zero, v)], axis=0)


def one_pair(v):
    return jnp.where(first_head(), v[:T], v[T:])


def stagger(count, stages):
    for n in range(count + len(stages) - 1):
        for s, stage in enumerate(stages):
            if 0 <= n - s < count:
                stage(n - s, (n - s) % 4)


def place_of(n):
    return n // PAIRS, n % PAIRS, (tile_at(n // PAIRS), tile_at(n % PAIRS))


def attend(q, k, v, p, ctx, spans, raw):
    def score(n, slot):
        i, j, at = place_of(n)
        raw[slot] = nt(k[at], two_heads(q[at]))

    def softmax(n, slot):
        i, j, at = place_of(n)
        s = jnp.where(causal(spans[i]), raw[slot] * SCALE, NEG)
        e = jnp.exp(s - jnp.max(s, axis=0, keepdims=True))
        p[i, j] = (e * (1.0 / jnp.sum(e, axis=0, keepdims=True))).astype(BF)

    def mix(n, slot):
        i, j, at = place_of(n)
        ctx[at] = one_pair(tn(p[i, j], v[at])).astype(BF)

    stagger(len(spans) * PAIRS, (score, softmax, mix))


def attend_back(tiles, q, k, v, p, dctx, dq, dk, dv, wide, raw, ds):
    def score(n, slot):
        i, j, at = place_of(n)
        wide[slot] = two_heads(dctx[at])
        raw[slot] = nt(v[at], wide[slot])

    def softmax(n, slot):
        i, j, at = place_of(n)
        pf, dp = p[i, j].astype(F32), raw[slot]
        ds[slot] = (pf * (dp - jnp.sum(pf * dp, axis=0, keepdims=True))).astype(BF)
        dv[at] = nn(p[i, j], wide[slot]).astype(BF)

    def mix(n, slot):
        i, j, at = place_of(n)
        dk[at] = (nn(ds[slot], two_heads(q[at])) * SCALE).astype(BF)
        dq[at] = (one_pair(tn(ds[slot], k[at])) * SCALE).astype(BF)

    stagger(tiles * PAIRS, (score, softmax, mix))


FORE = [((4, T, 2 * T), F32)]
BACK = [((4, 2 * T, T), BF), ((4, T, 2 * T), F32), ((4, T, 2 * T), BF)]


def gelu_both(u):
    c = 0.7978845608028654
    u2 = u * u
    t = jnp.tanh(c * u * (1.0 + 0.044715 * u2))
    half = 0.5 * (1.0 + t)
    slope = half + 0.5 * u * (1.0 - t * t) * (c * (1.0 + 3.0 * 0.044715 * u2))
    return u * half, slope


def tile_at(i):
    return slice(i * T, (i + 1) * T)


SPANS = (128, 128, 64, 32)


def forward_rows(x_ref, g1, wq, wk, wv, wo, n1, q, k, v, p, ctx, spans, raw, ready):
    xf = x_ref[...].astype(F32)
    n1[...] = (xf * inv_rms(xf) * row(g1)).astype(BF)
    for i, (out, w) in enumerate(((q, wq), (k, wk), (v, wv))):
        ready(i)
        out[...] = nn(n1[...], w[...]).astype(BF)
    attend(q, k, v, p, ctx, spans, raw)
    ready(3)
    return xf, nn(ctx[...], wo[...])


def pick_kernel(
    h_eighths, h_picks, h_tokens, h_cot, h_router, h_wq,
    xr, cr, dm, mine, other, tokens, cot, wq,
    eighths, picks, w_router, sem,
):
    pairs = (
        (h_eighths, eighths), (h_picks, picks), (h_tokens, tokens),
        (h_router, w_router), (h_cot, cot), (h_wq, wq),
    )
    loads = [pltpu.make_async_copy(h, v, sem.at[i]) for i, (h, v) in enumerate(pairs)]
    for load in loads:
        load.start()
    for load in loads[:5]:
        load.wait()
    s = lax.axis_index("seq")
    core = lax.axis_index("mlp") % 2
    eye = iota((T, T), 0) == iota((T, T), 1)
    for j in range(2):
        n = eighths[2 * s + j] * BLOCK
        col = jnp.sum(jnp.where(eye, picks[j : j + 1, :], 0), axis=1, keepdims=True)
        hot = (iota((T, 2 * T), 1) == col) & (iota((T, 2 * T), 0) < n)
        hot = jnp.where(hot, 1.0, 0.0).astype(BF)
        span = slice(2 * T * j, 2 * T * (j + 1))
        x = nn(hot, tokens[span, :])
        c = nn(hot, cot[span, :])
        gate = jnp.sum(x * row(w_router), axis=-1, keepdims=True)
        d = (gate.astype(BF).astype(F32) * c).astype(BF)
        xr[tile_at(j), :] = x.astype(BF)
        cr[tile_at(j), :] = c.astype(BF)
        dm[tile_at(j), :] = d

        for out, own in ((mine, core == j), (other, core != j)):

            @pl.when(own)
            def _():
                out[:T, :] = x.astype(BF)
                out[T : 2 * T, :] = d
    loads[5].wait()


def own_kernel(
    xr, dm, wq, hg1, hg2, hk, hv, ho, hup, hdown,
    keep, send, q, k, v, p, att, act, wk, wv, wo, wup, wdown,
    n1, ctx, n2, dup, raw, g1, g2, sem,
):
    core = lax.axis_index("mlp") % 2
    pairs = ((hg1, g1), (hk, wk), (hv, wv), (ho, wo), (hup, wup), (hdown, wdown), (hg2, g2))
    loads = [pltpu.make_async_copy(h, w, sem.at[i]) for i, (h, w) in enumerate(pairs)]
    for i in (0, 1, 2, 6):
        loads[i].start()
    loads[0].wait()

    def ready(i):
        if i == 0:
            for j in (3, 4, 5):
                loads[j].start()
        else:
            loads[i].wait()

    xf, attn = forward_rows(xr, g1, wq, wk, wv, wo, n1, q, k, v, p, ctx, (T, T), raw, ready)
    loads[6].wait()
    att[...] = attn
    mid = xf + attn
    n2[...] = (mid * inv_rms(mid) * row(g2)).astype(BF)
    loads[4].wait()
    a, slope = gelu_both(nn(n2[...], wup[...]))
    act[...] = a.astype(BF)
    loads[5].wait()
    dup[...] = (slope * nt(dm[...], wdown[...])).astype(BF)
    share(core, nt(dup[...], wup[...]), keep, send)


def share(core, both, keep, send):
    for j in range(2):

        @pl.when(core == j)
        def _():
            keep[...] = both[tile_at(j), :]
            send[...] = both[tile_at(1 - j), :].astype(BF)


def own_out_kernel(act, wdown, keep, send):
    share(lax.axis_index("mlp") % 2, nn(act[...], wdown[...]), keep, send)


def middle_kernel(dna, dnb, xr, cr, ac, g2, w_router, dattn, dmid_out, small):
    core = lax.axis_index("mlp") % 2
    rows = pl.ds(core * T, T)
    x = xr[rows, :].astype(F32)
    gate = jnp.sum(x * row(w_router), axis=-1, keepdims=True)
    gate = gate.astype(BF).astype(F32)
    mid = x + ac[rows, :]
    r = inv_rms(mid)
    unit = mid * r
    dn = dna[...].astype(F32) + dnb[...].astype(F32)
    small[...] = jnp.sum(dn * unit, axis=0, keepdims=True)
    scaled = dn * row(g2)
    dmid = r * (scaled - unit * jnp.mean(scaled * unit, axis=-1, keepdims=True))
    dmid_out[...] = dmid
    dattn[:T, :] = (gate * cr[rows, :].astype(F32) + dmid).astype(BF)


def own_back_kernel(
    dattn, dmid, small_in, moa, mob, xr, cr, ac, qc, kc, vc, pc, g1, w_router, wq, wk, wv, wo,
    delta, back, misc, dctx, dq, dk, dv, *work,
):
    core = lax.axis_index("mlp") % 2
    rows = pl.ds(core * T, T)
    x = xr[rows, :].astype(F32)
    wr = row(w_router)
    gate = jnp.sum(x * wr, axis=-1, keepdims=True).astype(BF).astype(F32)
    branch = ac[rows, :] + (moa[...].astype(F32) + mob[...].astype(F32))
    gg = jnp.sum(cr[rows, :].astype(F32) * branch, axis=-1, keepdims=True).astype(BF)
    delta[...] = (gate * branch).astype(BF)
    dctx[...] = nt(dattn[:T, :], wo[...]).astype(BF)
    q, k, v = (ref.at[rows, :] for ref in (qc, kc, vc))
    attend_back(1, q, k, v, pc.at[pl.ds(core, 1)], dctx, dq, dk, dv, *work)
    dn = nt(dq[...], wq[...]) + nt(dk[...], wk[...]) + nt(dv[...], wv[...])
    r = inv_rms(x)
    unit = x * r
    scaled = dn * row(g1)
    dx = r * (scaled - unit * jnp.mean(scaled * unit, axis=-1, keepdims=True))
    back[...] = (dmid[...] + dx).astype(BF)
    eye = iota((T, T), 0) == iota((T, T), 1)
    across = jnp.sum(jnp.where(eye, gg.astype(F32), 0.0), axis=0, keepdims=True)
    total = jnp.concatenate(
        [
            jnp.sum(gg.astype(F32) * x, axis=0, keepdims=True),
            jnp.sum(dn * unit, axis=0, keepdims=True),
            small_in[...],
            jnp.concatenate([across, jnp.zeros((1, D - T), F32)], axis=1),
            jnp.zeros((12, D), F32),
        ],
        axis=0,
    )
    high = total.astype(BF)
    misc[:16, :] = high
    misc[16:, :] = (total - high.astype(F32)).astype(BF)


def place_kernel(
    eighths, picks, w_router, delta, back, misc, delta_o, back_o, misc_o, tokens, cot,
    h_mixed, h_grad, mixed, grad, sem,
):
    s = lax.axis_index("seq")
    core = lax.axis_index("mlp") % 2
    wr = row(w_router)
    spans = [slice(2 * T * j, 2 * T * (j + 1)) for j in range(2)]
    stores = []
    eye = iota((T, T), 0) == iota((T, T), 1)
    for j, span in enumerate(spans):
        n = eighths[2 * s + j] * BLOCK
        hot = (iota((2 * T, T), 0) == picks[j : j + 1, :]) & (iota((2 * T, T), 1) < n)
        hot = jnp.where(hot, 1.0, 0.0).astype(BF)
        mine = core == j
        gg = jnp.where(mine, misc[3:4, :T], misc_o[3:4, :T]).astype(F32)
        gg = jnp.sum(jnp.where(eye, gg, 0.0), axis=1, keepdims=True)
        gg = nn(hot, jnp.broadcast_to(gg, (T, T)).astype(BF))[:, :1]
        forth = nn(hot, jnp.where(mine, delta[...], delta_o[...]))
        down = nn(hot, jnp.where(mine, back[...], back_o[...]))
        mixed[span, :] = (tokens[span, :].astype(F32) + forth).astype(BF)
        grad[span, :] = (cot[span, :].astype(F32) + (down + gg * wr)).astype(BF)
        for i, (v, h) in enumerate(((mixed, h_mixed), (grad, h_grad))):
            stores.append(pltpu.make_async_copy(v.at[span], h.at[span], sem.at[2 * j + i]))
            stores[-1].start()
    for store in stores:
        store.wait()


def dense_kernel(base, eighths, *refs):
    same, cross, dense, tile = refs[:4], refs[4:8], refs[8], refs[9]
    s = lax.axis_index("seq")
    core = lax.axis_index("mlp") % 2
    pos = s % 4
    first = (s // 4) * GROUP
    size = [eighths[first + i] for i in range(GROUP)]
    start = []
    for i in range(GROUP):
        total = jnp.int32(0)
        for j in range(GROUP):
            ahead = (size[j] >= size[i]) if j < i else (size[j] > size[i])
            if j != i:
                total = total + jnp.where(ahead, size[j], 0)
        start.append(total)

    def of(values, at):
        out = values[0]
        for i in range(1, GROUP):
            out = jnp.where(at == i, values[i], out)
        return out

    def put(src, seq):
        count, to = of(size, seq), of(start, seq)

        def move(first, last):
            dst = pl.multiple_of((to + first) * BLOCK, BLOCK)
            span = (last - first) * BLOCK
            dense[pl.ds(dst, span), :] = src[base + first * BLOCK : base + last * BLOCK, :]

        move(0, 1)
        pl.when(count >= 2)(lambda: move(1, 2))
        pl.when(count >= 4)(lambda: move(2, 4))

    for i in range(4):
        put(same[i], 2 * (pos ^ i) + core)
        put(cross[i], 2 * (pos ^ i) + 1 - core)
    tile[:T, :] = dense[pl.ds(pl.multiple_of((2 * (pos % 2) + core) * T, T), T), :]


def relay_kernel(*refs):
    n = len(refs) // 2
    for src, out in zip(refs[:n], refs[n:]):
        size = min(src.shape[0], out.shape[0]) // T * T
        out[:size, :] = src[:size, :]


def join_kernel(z, y, zc, yc, dense):
    pos = lax.axis_index("seq") % 2
    core = lax.axis_index("mlp") % 2
    for half, same, cross in ((pos, z, zc), (1 - pos, y, yc)):
        for src, at in ((same, 2 * half + core), (cross, 2 * half + 1 - core)):
            dense[pl.ds(pl.multiple_of(at * T, T), T), :] = src[:T, :]


def all_forward_kernel(x, g1, g2, wq, wk, wv, wo, n1, q, k, v, p, ctx, n2, raw):
    xf, attn = forward_rows(x, g1, wq, wk, wv, wo, n1, q, k, v, p, ctx, SPANS, raw, lambda i: None)
    mid = xf + attn
    n2[...] = (mid * inv_rms(mid) * row(g2)).astype(BF)


def thirds():
    step = D // 3
    return [slice(j * step, (j + 1) * step) for j in range(3)]


def grad_out(outs, bufs, tmp, sem, parts, olds, first):
    stores = []
    for i, (left, right) in enumerate(parts):
        for j, at in enumerate(thirds()):
            tmp[j][...] = tn(left[:, at], right[...])
            bufs[i][at, :] = tmp[j][...] + olds[i][at, :]
            stores.append(pltpu.make_async_copy(bufs[i].at[at], outs[i].at[at], sem.at[first + 3 * i + j]))
            stores[-1].start()
    return stores


def mlp_rows(n2, dm, wup, wdown, act, dup):
    a, slope = gelu_both(nn(n2[...], wup[...]))
    act[...] = a.astype(BF)
    dup[...] = (slope * nt(dm[...], wdown[...])).astype(BF)


def first_mlp_kernel(n2, dm, wup, wdown, gup, gdown, act, dup):
    mlp_rows(n2, dm, wup, wdown, act, dup)
    for out, left, right in ((gdown, act, dm), (gup, n2, dup)):
        for at in thirds():
            out[at, :] = tn(left[:, at], right[...])


def last_mlp_kernel(n2, dm, wup, wdown, gup_a, gdown_a, gup, gdown, act, dup, b0, b1, t0, t1, t2, sem):
    mlp_rows(n2, dm, wup, wdown, act, dup)
    parts = ((act, dm), (n2, dup))
    for store in grad_out((gdown, gup), (b0, b1), (t0, t1, t2), sem, parts, (gdown_a, gup_a), 0):
        store.wait()


def back_rows(dattn, q, k, v, p, wo, dq, dk, dv, dctx, work):
    dctx[...] = nt(dattn[...], wo[...]).astype(BF)
    attend_back(4, q, k, v, p, dctx, dq, dk, dv, *work)


def first_back_kernel(dattn, q, k, v, p, wo, dq, dk, dv, dctx, *work):
    back_rows(dattn, q, k, v, p, wo, dq, dk, dv, dctx, work)


def first_grad_kernel(dattn, n1, ctx, dq, dk, dv, gq, gk, gv, go):
    for out, left, right in ((go, ctx, dattn), (gv, n1, dv), (gk, n1, dk), (gq, n1, dq)):
        for at in thirds():
            out[at, :] = tn(left[:, at], right[...])


def last_back_kernel(
    dattn, q, k, v, p, wo, n1, ctx, gq_a, gk_a, gv_a, go_a,
    gq, gk, gv, go, dq, dk, dv, dctx, w0, w1, w2, b0, b1, b2, b3, t0, t1, t2, sem,
):
    stores = grad_out((go,), (b0,), (t0, t1, t2), sem, ((ctx, dattn),), (go_a,), 0)
    back_rows(dattn, q, k, v, p, wo, dq, dk, dv, dctx, (w0, w1, w2))
    parts, olds = ((n1, dv), (n1, dk), (n1, dq)), (gv_a, gk_a, gq_a)
    stores += grad_out((gv, gk, gq), (b1, b2, b3), (t0, t1, t2), sem, parts, olds, 3)
    for store in stores:
        store.wait()


def fold_half_kernel(keep, came, half):
    half[...] = (keep[...] + came[...].astype(F32)).astype(BF)


def fold_kernel(a, b, out):
    out[...] = a[...] + b[...]


def halves(total):
    high = total.astype(BF).astype(F32)
    return high, (total - high).astype(BF).astype(F32)


def keep(total, rows, out):
    high, low = halves(total)
    rows[...] = jnp.concatenate([high, low], axis=0).astype(BF)
    out[...] = high + low


def read(rows):
    both = rows[...].astype(F32)
    return both[:8] + both[8:]


def unpack_kernel(mine, other, tile, out_tile, out):
    def whole(ref):
        return ref[:8, :].astype(F32) + ref[16:24, :].astype(F32)

    out_tile[:T, :] = tile[:T, :]
    keep(whole(mine) + whole(other), out_tile.at[T : T + 16], out)


def relay_fold_kernel(tile, small, out_tile, out):
    out_tile[:T, :] = tile[:T, :]
    keep(small[...] + read(tile.at[T : T + 16]), out_tile.at[T : T + 16], out)


def last_fold_kernel(a, b, o0, o1, o2):
    v = a[...] + b[...]
    for i, out in enumerate((o0, o1, o2)):
        out[...] = v[i]


LIMIT = {
    "pick_kernel": 8, "own_kernel": 24, "middle_kernel": 8, "own_back_kernel": 16,
    "place_kernel": 10, "dense_kernel": 8, "join_kernel": 6, "all_forward_kernel": 14,
    "first_mlp_kernel": 12, "last_mlp_kernel": 16, "first_back_kernel": 10, "last_back_kernel": 22,
    "first_grad_kernel": 8,
    "fold_half_kernel": 4, "own_out_kernel": 6, "fold_kernel": 4, "unpack_kernel": 4, "relay_fold_kernel": 4, "last_fold_kernel": 4,
    "relay_kernel": 4,
}


VM = pl.BlockSpec(memory_space=pltpu.VMEM)
SM = pl.BlockSpec(memory_space=pltpu.SMEM)
HB = pl.BlockSpec(memory_space=pltpu.HBM)
AN = pl.BlockSpec(memory_space=pl.ANY)


def call(
    kernel, ins, outs, scratch=(), scalars=0, after=(), through=(), hbm_in=0, hbm_out=False,
    sems=0,
):
    n, skip, m, t = len(ins), len(after), len(outs), len(through)
    name = getattr(kernel, "func", kernel).__name__

    def body(*refs):
        given, made = refs[n + skip : n + skip + t], refs[n + skip + t + m :][:t]
        for old, new in zip(given, made):
            new[...] = old[...]
        kernel(*refs[:n], *refs[n + skip + t :][:m], *refs[n + skip + t + m + t :])

    own = n - scalars - hbm_in
    return pl.pallas_call(
        body,
        name=name,
        out_shape=[jax.ShapeDtypeStruct(s, d) for s, d in outs]
        + [jax.ShapeDtypeStruct(v.shape, v.dtype) for v in through],
        in_specs=[SM] * scalars + [VM] * own + [HB] * hbm_in + [AN] * skip + [VM] * t,
        out_specs=[HB if hbm_out else VM] * m + [VM] * t,
        scratch_shapes=[like(v) for v in scratch]
        + ([pltpu.SemaphoreType.DMA((sems,))] if sems else []),
        compiler_params=pltpu.CompilerParams(vmem_limit_bytes=LIMIT[name] * MIB),
        cost_estimate=pl.CostEstimate(flops=1000, bytes_accessed=1000, transcendentals=0),
    )(*ins, *after, *through)


def like(v):
    if isinstance(v, tuple):
        return pltpu.VMEM(*v)
    return (pltpu.SMEM if v.dtype == jnp.int32 and v.ndim == 1 else pltpu.VMEM)(v.shape, v.dtype)


def far_off(v):
    return pltpu.with_memory_space_constraint(v, pltpu.HBM)


def swap(value, axis, mask):
    pairs = [(i, i ^ mask) for i in range(lax.axis_size(axis))]
    return lax.ppermute(value, axis, pairs)


def rows(n, t=BF):
    return ((n, D), t)


def probs(n):
    return ((n, PAIRS, T, 2 * T), BF)


def local(
    tokens, cotangent, picks, eighths, w_router, gain_attn, gain_mlp,
    wq, wk, wv, wo, wup, wdown,
):
    wr, g1, g2 = w_router, gain_attn, gain_mlp

    def relay(parts, after=(), through=()):
        sizes = [rows(v.shape[0] // T * T) for v in parts]
        return call(relay_kernel, parts, sizes, after=after)

    def dense(same, cross, base=0, after=(), through=(), pad=0):
        return call(
            functools.partial(dense_kernel, base), (eighths, *same, *cross),
            [rows(4 * T), rows(T + 8 * pad)], scalars=1, after=after, through=through,
        )

    def join(parts, after=()):
        return call(join_kernel, parts, [rows(4 * T)], after=after)[0]

    def core(v):
        return swap(v, "mlp", 1)

    def all_forward(x, after=(), through=()):
        return call(
            all_forward_kernel, (x, g1, g2, wq, wk, wv, wo),
            [rows(4 * T)] * 4 + [probs(4)] + [rows(4 * T)] * 2, FORE, after=after, through=through,
        )

    def fold(v, mask, after=()):
        return call(fold_kernel, (v, swap(v, "seq", mask)), [rows(8, F32)], after=after)[0]

    xr, cr, dm, mine, other, tokens, cotangent, wq = call(
        pick_kernel, [far_off(v) for v in (eighths, picks, tokens, cotangent, wr, wq)],
        [rows(2 * T)] * 3 + [rows(2 * T + XD), rows(2 * T)] + [rows(4 * T)] * 2 + [rows(D)],
        [eighths, picks, wr], hbm_in=6, sems=6,
    )
    near = [swap(mine, "seq", k) for k in (1, 2, 3)]
    keep_n, send_n, qc, kc, vc, pc, ac, act, wk, wv, wo, wup, wdown = call(
        own_kernel, (xr, dm, wq, *(far_off(v) for v in (g1, g2, wk, wv, wo, wup, wdown))),
        [rows(T, F32), rows(T)] + [rows(2 * T)] * 3
        + [probs(2), rows(2 * T, F32), rows(2 * T)] + [rows(D)] * 5,
        [rows(2 * T)] * 4 + FORE + [g1, g2], hbm_in=7, sems=7,
    )
    keep_m, send_m = call(own_out_kernel, (act, wdown), [rows(T, F32), rows(T)])
    (half_n,) = call(
        fold_half_kernel, (keep_n, core(send_n)), [rows(T)], after=(keep_m,)
    )
    (half_m,) = call(
        fold_half_kernel, (keep_m, core(send_m)), [rows(T)], after=(half_n,)
    )
    both_n = swap(half_n, "mlp", 2)
    dattn, dmid, small, half_m = call(
        middle_kernel, (half_n, both_n, xr, cr, ac, g2, wr),
        [rows(T + 16), rows(T, F32), ((1, D), F32)], through=(half_m,),
    )
    a1, a2, a3 = [swap(dattn, "seq", k) for k in (1, 2, 3)]
    both_m = swap(half_m, "mlp", 2)
    near = relay(near, after=(dattn,))
    same, cross = (mine, *near), (other, *(core(v) for v in near))
    x_a, x_tile = dense(same, cross, pad=1)
    far_x = swap(x_tile, "seq", 4)
    n1_a, q_a, k_a, v_a, p_a, ctx_a, n2_a = all_forward(x_a)
    res = call(
        own_back_kernel,
        (dattn, dmid, small, half_m, both_m, xr, cr, ac, qc, kc, vc, pc, g1, wr, wq, wk, wv, wo),
        [rows(T), rows(T), rows(32)], [rows(T)] * 4 + BACK, after=(n2_a,),
    )
    same_a = relay([dattn, a1, a2, a3], after=(res[0],))
    cross_a = [core(v) for v in same_a]
    d_a, d_tile = dense(same, cross, base=T, after=(same_a[0],))
    a_a, a_tile = dense(same_a, cross_a, after=(d_a,), pad=1)
    far_a = swap(a_tile, "seq", 4)
    (far_x,) = relay([far_x], after=(a_a,))
    near_x = swap(far_x, "seq", 1)
    dq_a, dk_a, dv_a, *res = call(
        first_back_kernel, (a_a, q_a, k_a, v_a, p_a, wo), [rows(4 * T)] * 3,
        [rows(4 * T)] + BACK, after=(far_x,), through=res,
    )
    other = [core(v) for v in res]
    ups = call(
        first_mlp_kernel, (n2_a, d_a, wup, wdown), [rows(D, F32)] * 2, [rows(4 * T)] * 2,
        after=(dq_a,),
    )
    d_tile, small = call(
        unpack_kernel, (res[2], other[2], d_tile), [rows(T + 16), rows(8, F32)], after=(ups[0],)
    )
    far_d = swap(d_tile, "seq", 4)
    mixed, grad_tokens, small = call(
        place_kernel, (eighths, picks, wr, *res, *other, tokens, cotangent),
        [rows(4 * T)] * 2, [rows(4 * T)] * 2, scalars=1, hbm_out=True, sems=4,
        through=(small,),
    )
    grads = call(
        first_grad_kernel, (a_a, n1_a, ctx_a, dq_a, dk_a, dv_a), [rows(D, F32)] * 4,
        after=(small,),
    )
    (far_a,) = relay([far_a], after=(grads[0],))
    near_a = swap(far_a, "seq", 1)
    far_x, near_x = relay([far_x, near_x], after=(far_a,))
    cross_x, next_x = core(far_x), core(near_x)
    n1_b, q_b, k_b, v_b, p_b, ctx_b, n2_b = all_forward(
        join((far_x, near_x, cross_x, next_x))
    )
    far_d, small = call(
        relay_fold_kernel, (far_d, small), [rows(T + 16), rows(8, F32)], after=(n2_b,)
    )
    near_d, cross_d = swap(far_d, "seq", 1), core(far_d)
    far_a, near_a = relay([far_a, near_a], after=(small,))
    cross_a, next_a = core(far_a), core(near_a)
    a_b = join((far_a, near_a, cross_a, next_a))
    gq, gk, gv, go, token = call(
        last_back_kernel, (a_b, q_b, k_b, v_b, p_b, wo, n1_b, ctx_b, *grads),
        [rows(D, F32)] * 4,
        [rows(4 * T)] * 4 + BACK + [rows(D, F32)] * 4 + [rows(D // 3, F32)] * 3,
        hbm_out=True, sems=12, through=(small,),
    )
    near_d, small = call(
        relay_fold_kernel, (near_d, small), [rows(T + 16), rows(8, F32)], after=(token,)
    )
    d_b = join((far_d, near_d, cross_d, core(near_d)))
    gup, gdown, token = call(
        last_mlp_kernel, (n2_b, d_b, wup, wdown, *ups), [rows(D, F32)] * 2,
        [rows(4 * T)] * 2 + [rows(D, F32)] * 2 + [rows(D // 3, F32)] * 3,
        hbm_out=True, sems=6, through=(small,),
    )
    mask = lax.axis_size("seq") // 2
    while mask > 4:
        small = fold(small, mask)
        mask //= 2
    smalls = call(
        last_fold_kernel, (small, swap(small, "seq", 2)), [((D,), F32)] * 3, after=(token,)
    )
    total = [gq, gk, gv, go, gup, gdown]
    mask = 8
    while mask < lax.axis_size("seq"):
        total = [g + swap(g, "seq", mask) for g in total]
        mask *= 2
    return (mixed, grad_tokens, *smalls, *total)


def solution(mesh):
    rows, cols, split, full = P("seq", None), P(None, "mlp"), P("mlp", None), P()
    return jax.shard_map(
        local,
        mesh=mesh,
        in_specs=(rows, rows, rows) + (full,) * 8 + (cols, split),
        out_specs=(rows, rows) + (full,) * 7 + (cols, split),
        check_vma=False,
    )
```
